32 devices in a mesh: dp: 8 (over z, x), dim: 4 (over y, core).
Axes of the slice: x: 2, y: 2, z: 4, core: 2. Of those that a mesh axis runs over, the one named last changes fastest.
Arguments:
- attribute_vectors: bfloat16 [128, 512, 256], P('dp', 'dim'), may hold values from -6 to 6
- upstream: bfloat16 [128, 512, 256], P('dp', 'dim'), may hold values from -6 to 6
- compress: bfloat16 [256, 64], replicated, may hold values from -0.375 to 0.375
- interact_proj: bfloat16 [64, 512], P(None, 'dim'), may hold values from -0.75 to 0.75
- linear_mix: bfloat16 [256, 256], replicated, may hold values from -0.375 to 0.375
- row_owner: int32 [32768, 1], P('dp'), may hold values from 0 to 7; in each aligned block of 4096 rows (0 to 4095, 4096 to 8191, ...) at most 2048 rows name the same one
- row_slot: int32 [32768], P('dp'), may hold values from 0 to 255
Outputs:
- table_grad: float32 [512, 2048], P('dim', 'dp')
The draws below stay inside these ranges and needn't reach their ends.
Inputs may be any that keep to these rules, and one draw needn't show every extreme that they name: `row_owner`: in each aligned block of 4096 rows (the rows of one device) no owner is named by more than 2048 rows, a bound that some block reaches.
All inputs are finite; a program needn't handle non-finite values.
Results may differ from the reference program's by a relative error of at most 0.0035.
Values may be sent and summed in bfloat16 or wider, within the bound.
No kernel may reach another device: no remote copies, remote signals or barrier semaphores. Data moves between devices by JAX's collectives and lax.ppermute only.
A program may use at most 64 MiB of HBM per device.

```python
import math
import jax
import jax.numpy as jnp
import numpy as np
from jax import lax

F = 256
D = 512
K = 64
B_DEV = 16
SHARD = 256
SAMPLES = 128
ROWS = 32768
CAP = 2048
N_DP = 8


def place_ends(result, stream_key, smallest, top_value):
    place = [jax.random.randint(jax.random.fold_in(stream_key, axis), (), 0, length) for axis, length in enumerate(result.shape)]
    main_axis = result.shape.index(max(result.shape))
    neighbour = place[:main_axis] + [(place[main_axis] + 1) % result.shape[main_axis]] + place[main_axis + 1:]
    return result.at[tuple(place)].set(smallest).at[tuple(neighbour)].set(top_value)


def block_scale(own_key, shape, shards, low, largest):
    def one(axis_at, parts):
        draws = jax.random.uniform(jax.random.fold_in(jax.random.fold_in(own_key, 6), axis_at), (parts,), jnp.float32, low / len(shards), largest / len(shards))
        return jnp.repeat(jnp.exp(draws), shape[axis_at] // parts).reshape((-1,) + (1,) * (len(shape) - axis_at - 1))

    gain = one(*shards[0])
    for cut in shards[1:]:
        gain = gain * one(*cut)
    return gain


def shared_out(stream_key, own, number, rows, amount, top, most, skew):
    order = jax.random.permutation(stream_key, amount)
    packed, usual = portions_of(amount, rows * top, most, skew, True), portions_of(amount, rows * top, most, skew, False)
    places = jnp.arange(amount)

    def named(lengths, rotation):
        used = int((lengths > 0).sum())
        fixed = max(1, used // 4)
        moved = fixed + (places - fixed + rotation * (used - fixed)) % max(1, amount - fixed)
        return jnp.zeros((amount,), jnp.int32).at[order[jnp.where(places < fixed, places, moved)]].set(jnp.asarray(lengths, jnp.int32))

    lengths = jnp.where(number % 4 == 0, named(packed, number // 4), named(usual, number - number // 4 - 1))
    mixed = jax.random.permutation(jax.random.fold_in(own, 3), amount)
    giver, taker = mixed[0:amount // 2 * 2:2], mixed[1:amount // 2 * 2:2]
    margin = jnp.minimum(lengths[giver] - 1, most - lengths[taker]) // 2
    margin = jnp.where((giver == order[0]) | (taker == order[0]) | (lengths[taker] == 0), 0, jnp.maximum(margin, 0))
    moved = jax.random.randint(jax.random.fold_in(own, 4), (amount // 2,), 0, 1 << 20) % (margin + 1)
    lengths = lengths.at[giver].add(-moved).at[taker].add(moved)
    items = jnp.searchsorted(jnp.cumsum(lengths), jnp.arange(rows * top), side="right").astype(jnp.int32)
    listing = items.reshape(top, rows).T
    listing = listing[jax.random.permutation(jax.random.fold_in(own, 1), rows)]
    rotation = jax.random.randint(jax.random.fold_in(own, 2), (rows, 1), 0, top)
    return jnp.take_along_axis(listing, (jnp.arange(top)[None, :] + rotation) % top, axis=1)


def portions_of(number_of, total, most, slope, full):
    portions = [(1 << 20) // math.isqrt(standing ** slope) + 1 for standing in range(1, number_of + 1)]
    largest = most if full else min(most, max(-(-total // number_of), total * portions[0] // sum(portions)))
    least = 1 if total - largest >= number_of - 1 else 0
    holding, surplus = [largest] + [least] * (number_of - 1), total - largest - least * (number_of - 1)
    while surplus > 0:
        free = [i for i in range(1, number_of) if holding[i] < largest] or [i for i in range(1, number_of) if holding[i] < most]
        mass, budget = sum([portions[i] for i in free]), surplus
        for i in free:
            extra = min(most - holding[i], max(1, budget * portions[i] // mass), surplus)
            holding[i] = holding[i] + extra
            surplus = surplus - extra
    return np.array(holding)


def bell_draw(key, dims, scale, reach, pieces=(), kind=jnp.bfloat16):
    loudness = block_scale(key, dims, pieces, -0.22, 0.18) if pieces else 1.0
    drawn = jax.random.normal(key, dims, jnp.float32) * scale * loudness
    return jnp.minimum(jnp.maximum(drawn, -reach), reach).astype(kind)


def setup_inputs(seed: int = 0) -> dict:
    splits = jax.random.split(jax.random.key(seed), 8)
    attribute_vectors = bell_draw(splits[0], (SAMPLES, D, F), 1.0, 6.0, ((0, 8), (1, 4)))
    upstream = bell_draw(splits[1], (SAMPLES, D, F), 1.0, 6.0, ((0, 8), (1, 4)))
    compress = bell_draw(splits[2], (F, K), F ** -0.5, 0.375)
    interact_proj = bell_draw(splits[3], (K, D), K ** -0.5, 0.75, ((1, 4),))
    linear_mix = bell_draw(splits[4], (F, F), F ** -0.5, 0.375)
    row_owner_keys = jax.random.split(jax.random.fold_in(splits[5], 1), ROWS // (B_DEV * F))
    row_owner_turns = jax.random.permutation(jax.random.fold_in(splits[5], 3), ROWS // (B_DEV * F))
    row_owner = jax.vmap(lambda own, number: shared_out(jax.random.fold_in(splits[5], 2), own, number, B_DEV * F, N_DP, 1, CAP, 2))(row_owner_keys, row_owner_turns).reshape((ROWS, 1))
    row_slot = place_ends(jax.random.randint(splits[6], (ROWS,), 0, SHARD), jax.random.fold_in(splits[6], 1), 0, SHARD - 1).astype(jnp.int32)
    return dict(attribute_vectors=attribute_vectors, upstream=upstream, compress=compress, interact_proj=interact_proj, linear_mix=linear_mix, row_owner=row_owner, row_slot=row_slot)


def layer_back(totals, upstream_n):
    centred = totals - lax.optimization_barrier(jnp.mean(totals, axis=-1, keepdims=True))
    inverse = 1.0 / jnp.sqrt(lax.optimization_barrier(jnp.mean(centred * centred, axis=-1, keepdims=True)) + 1e-05)
    normed = centred * inverse
    return inverse * (upstream_n - lax.optimization_barrier(jnp.mean(upstream_n, axis=-1, keepdims=True)) - normed * lax.optimization_barrier(jnp.mean(upstream_n * normed, axis=-1, keepdims=True)))

def reference(attribute_vectors, upstream, compress, interact_proj, linear_mix, row_owner, row_slot):
    stratum_sources = attribute_vectors.astype(jnp.float32)
    grads = upstream.astype(jnp.float32)
    compressor_wide_weight = compress.astype(jnp.float32)
    reduced_lookup_vectors = jnp.einsum('qy,piq->pyi', compressor_wide_weight, stratum_sources).astype(jnp.bfloat16)
    reduced_broad_entries = reduced_lookup_vectors.astype(jnp.float32)
    attribute_aggregates = jnp.einsum('pzt,pvz->ptv', stratum_sources, reduced_broad_entries)
    normed_grad = jnp.einsum('bdf,kd->bfk', grads, interact_proj.astype(jnp.float32))
    pairwise_gradient = layer_back(attribute_aggregates, normed_grad).astype(jnp.bfloat16).astype(jnp.float32)
    leading_product_term = jnp.einsum('sxh,shl->slx', pairwise_gradient, reduced_broad_entries)
    compressor_gradient = jnp.einsum('itm,ipt->imp', pairwise_gradient, stratum_sources).astype(jnp.bfloat16)
    trailing_product_term = jnp.einsum('hu,zux->zxh', compressor_wide_weight, compressor_gradient.astype(jnp.float32))
    linear_term = jnp.einsum('bdg,fg->bdf', grads, linear_mix.astype(jnp.float32))
    feature_grad = (grads + linear_term + leading_product_term + trailing_product_term).astype(jnp.bfloat16)
    grad_rows = jnp.transpose(feature_grad, (0, 2, 1)).reshape(ROWS, D).astype(jnp.float32)
    targets = (row_owner[:, 0] * SHARD + row_slot).astype(jnp.int32)
    table = jax.ops.segment_sum(grad_rows, targets, num_segments=N_DP * SHARD)
    return jnp.transpose(table)
```

```python
import functools

import jax
import jax.numpy as jnp
from jax import lax
from jax.experimental import pallas as pl
from jax.experimental.pallas import tpu as pltpu
from jax.sharding import PartitionSpec as P

SHARD = 256
F32, BF16 = jnp.float32, jnp.bfloat16


def dot_nt(a, b):
    return lax.dot_general(a, b, (((1,), (1,)), ((), ())), preferred_element_type=F32)


def dot_nn(a, b):
    return lax.dot_general(a, b, (((1,), (0,)), ((), ())), preferred_element_type=F32)


def transposed(ref):
    return ref[...].astype(F32).T.astype(BF16)


def partial_sums_kernel(pieces_ref, av_ref, up_ref, compress_ref, proj_ref, send_ref, keep_ref, comp_t):
    step = pl.program_id(0)

    @pl.when(step == 0)
    def _():
        comp_t[...] = transposed(compress_ref)

    count = av_ref.shape[0]
    half = pl.num_programs(0) // 2
    rank = comp_t.shape[0]
    for b in range(count):
        reduced = dot_nt(comp_t[...], av_ref[b]).astype(BF16)
        sums = dot_nn(reduced, av_ref[b])
        sums = sums - jnp.mean(sums, axis=0, keepdims=True)
        grads = dot_nn(proj_ref[...], up_ref[b])
        grads = grads - jnp.mean(grads, axis=0, keepdims=True)

        @pl.when(step < half)
        def _():
            send_ref[b, :rank] = sums
            send_ref[b, rank:] = grads

        @pl.when(step >= half)
        def _():
            keep_ref[b, :rank] = sums
            keep_ref[b, rank:] = grads


def partial_sums(pieces, av, up, compress, proj):
    samples, width, features = av.shape
    count = pieces.shape[0]
    piece = samples // count
    rank = compress.shape[1]
    half = count // 2
    block = (piece, width, features)
    out_block = (piece, 2 * rank, features)
    return pl.pallas_call(
        partial_sums_kernel,
        grid_spec=pltpu.PrefetchScalarGridSpec(
            num_scalar_prefetch=1,
            grid=(count,),
            in_specs=[
                pl.BlockSpec(block, lambda i, q: (q[i], 0, 0)),
                pl.BlockSpec(block, lambda i, q: (q[i], 0, 0)),
                pl.BlockSpec(compress.shape, lambda i, q: (0, 0)),
                pl.BlockSpec(proj.shape, lambda i, q: (0, 0)),
            ],
            out_specs=[
                pl.BlockSpec(out_block, lambda i, q: (jnp.minimum(i, half - 1), 0, 0)),
                pl.BlockSpec(out_block, lambda i, q: (jnp.maximum(i - half, 0), 0, 0)),
            ],
            scratch_shapes=[pltpu.VMEM((rank, features), BF16)],
        ),
        out_shape=[jax.ShapeDtypeStruct((half * piece, 2 * rank, features), F32)] * 2,
        compiler_params=pltpu.CompilerParams(vmem_limit_bytes=16 * 2**20),
        name="partial_sums",
    )(pieces, av, up, compress, proj)


def layer_back_kernel(keep_ref, got_ref, pair_ref):
    rank = keep_ref.shape[1] // 2
    for b in range(keep_ref.shape[0]):
        total = keep_ref[b] + got_ref[b].astype(F32)
        centred, grads = total[:rank], total[rank:]
        inverse = 1.0 / jnp.sqrt(jnp.mean(centred * centred, axis=0, keepdims=True) + 1e-05)
        normed = centred * inverse
        moment = jnp.mean(grads * normed, axis=0, keepdims=True)
        pair_ref[b] = (inverse * (grads - normed * moment)).astype(BF16)


def layer_back(keep, got):
    samples, twice, features = keep.shape
    return pl.pallas_call(
        layer_back_kernel,
        out_shape=jax.ShapeDtypeStruct((samples, twice // 2, features), BF16),
        compiler_params=pltpu.CompilerParams(vmem_limit_bytes=16 * 2**20),
        name="layer_back",
    )(keep, got)


def table_kernel(owners, starts, pieces_ref, av_ref, up_ref, compress_ref, mix_ref, owner_ref, slot_ref, *rest):
    pair_refs = rest[: len(starts)]
    out_ref, comp_pair, masked, onehot, total = rest[len(starts):]
    step = pl.program_id(0)
    count, width, features = av_ref.shape
    rank = compress_ref.shape[1]

    @pl.when(step == 0)
    def _():
        comp_t = transposed(compress_ref)
        for b in range(count):
            comp_pair[b, :rank] = comp_t
            comp_pair[b, 2 * rank:] = comp_t
        total[...] = jnp.zeros_like(total)

    for pair_ref, start in zip(pair_refs, starts):
        for at in range(pair_ref.shape[0] // count):
            @pl.when(step == start + at)
            def _():
                comp_pair[:, rank:2 * rank] = pair_ref[at * count:(at + 1) * count]

    up = up_ref[...].reshape(count * width, features)
    linear = up.astype(F32) + dot_nt(up, mix_ref[...])
    first = pieces_ref[step] * count
    slots = lax.broadcasted_iota(jnp.int32, (SHARD, features), 0)
    for b in range(count):
        both = dot_nt(av_ref[b], comp_pair[b, :2 * rank]).astype(BF16)
        grad = linear[b * width:(b + 1) * width] + dot_nn(both, comp_pair[b, rank:])
        grad = grad.astype(BF16)
        owner = owner_ref[pl.ds(first + b, 1), :]
        columns = slice(b * features, (b + 1) * features)
        for o in range(owners):
            mask = jnp.where(owner == o, 1.0, 0.0).astype(BF16)
            masked[o * width:(o + 1) * width, columns] = grad * mask
        hit = slots == slot_ref[pl.ds(first + b, 1), :]
        onehot[:, columns] = jnp.where(hit, 1.0, 0.0).astype(BF16)
    total[...] += dot_nt(masked[...], onehot[...])

    @pl.when(step == pl.num_programs(0) - 1)
    def _():
        out_ref[...] = total[...].reshape(out_ref.shape).astype(BF16)


def table_partial(owners, pieces, av, up, compress, mix, owner, slot, pairs):
    samples, width, features = av.shape
    count = pieces.shape[0]
    piece = samples // count
    rank = compress.shape[1]
    starts, start = [], 0
    for pair in pairs:
        starts.append(start)
        start += pair.shape[0] // piece
    block = pl.BlockSpec((piece, width, features), lambda i, q: (q[i], 0, 0))

    def whole(a):
        return pl.BlockSpec(a.shape, lambda i, q: (0,) * a.ndim)

    return pl.pallas_call(
        functools.partial(table_kernel, owners, starts),
        grid_spec=pltpu.PrefetchScalarGridSpec(
            num_scalar_prefetch=1,
            grid=(count,),
            in_specs=[block, block] + [whole(a) for a in (compress, mix, owner, slot, *pairs)],
            out_specs=pl.BlockSpec((owners, width, SHARD), lambda i, q: (0, 0, 0)),
            scratch_shapes=[
                pltpu.VMEM((piece, 3 * rank, features), BF16),
                pltpu.VMEM((owners * width, piece * features), BF16),
                pltpu.VMEM((SHARD, piece * features), BF16),
                pltpu.VMEM((owners * width, SHARD), F32),
            ],
        ),
        out_shape=jax.ShapeDtypeStruct((owners, width, SHARD), BF16),
        compiler_params=pltpu.CompilerParams(vmem_limit_bytes=24 * 2**20),
        name="table_partial",
    )(pieces, av, up, compress, mix, owner, slot, *pairs)


def shards(attribute_vectors, upstream, compress, interact_proj, linear_mix, row_owner, row_slot):
    owners = lax.axis_size("dp")
    peers = lax.axis_size("dim")
    me = lax.axis_index("dim")
    samples, width, features = attribute_vectors.shape
    piece = samples // peers

    def swap(x, bit):
        return lax.ppermute(x, "dim", [(i, i ^ bit) for i in range(peers)])

    bits = [1 << t for t in range(peers.bit_length() - 1)]
    order = [0]
    for bit in reversed(bits):
        order += [j ^ bit for j in order]
    order = jnp.asarray(order, jnp.int32)
    pieces = order ^ me.astype(jnp.int32)
    send_first = jnp.roll(order, peers // 2) ^ me.astype(jnp.int32)

    send, keep = partial_sums(send_first, attribute_vectors, upstream, compress, interact_proj)
    got = swap(send, bits[0])
    for bit in bits[1:]:
        keep = keep + got.astype(F32)
        half = keep.shape[0] // 2
        got = swap(keep[half:].astype(BF16), bit)
        keep = keep[:half]
    pair = layer_back(keep, got)
    pairs = [pair]
    for bit in reversed(bits):
        pairs += [swap(jnp.concatenate(pairs) if len(pairs) > 1 else pairs[0], bit)]

    table = table_partial(
        owners,
        pieces,
        attribute_vectors,
        upstream,
        compress,
        linear_mix,
        row_owner.reshape(samples, features),
        row_slot.reshape(samples, features),
        pairs,
    )
    got = lax.all_to_all(table, "dp", split_axis=0, concat_axis=0, tiled=True)
    return jnp.sum(got.astype(F32), axis=0)


def solution(mesh):
    placed = (
        P("dp", "dim", None),
        P("dp", "dim", None),
        P(),
        P(None, "dim"),
        P(),
        P("dp", None),
        P("dp"),
    )
    return jax.shard_map(
        shards, mesh=mesh, in_specs=placed, out_specs=P("dim", "dp"), check_vma=False
    )
```

```python
import functools

import jax
import jax.numpy as jnp
from jax import lax
from jax.experimental import pallas as pl
from jax.experimental.pallas import tpu as pltpu
from jax.sharding import PartitionSpec as P

SHARD = 256
F32, BF16 = jnp.float32, jnp.bfloat16
LIMIT = 20 * 2**20
LOAD_LIMIT = 50 * 2**20
VMEM = pl.BlockSpec(memory_space=pltpu.VMEM)


def dot_nt(a, b):
    return lax.dot_general(a, b, (((1,), (1,)), ((), ())), preferred_element_type=F32)


def dot_nn(a, b):
    return lax.dot_general(a, b, (((1,), (0,)), ((), ())), preferred_element_type=F32)


def bits_of(size):
    return [1 << t for t in range(size.bit_length() - 1)]


def halves(bits):
    numbers = [0]
    for bit in reversed(bits):
        numbers += [n ^ bit for n in numbers]
    return numbers


def cost(flops, moved):
    return pl.CostEstimate(flops=flops, bytes_accessed=moved, transcendentals=0)


def width_sums(comp_t_ref, proj_ref, av_ref, up_ref, places, out_refs):
    rank = comp_t_ref.shape[0]
    for n, place in enumerate(places):
        out_ref, at = out_refs[2 * n // len(places)], n % (len(places) // 2)
        reduced = dot_nt(comp_t_ref[...], av_ref[place]).astype(BF16)
        sums = dot_nn(reduced, av_ref[place])
        out_ref[at, :rank] = sums - jnp.mean(sums, axis=0, keepdims=True)
        grads = dot_nn(proj_ref[...], up_ref[place])
        out_ref[at, rank:] = grads - jnp.mean(grads, axis=0, keepdims=True)


def load_kernel(order, groups, av_hbm, up_hbm, comp_t_ref, proj_ref, send_ref, keep_ref, av_ref, up_ref, av_sem, up_sem):
    me = lax.axis_index("dim")
    samples = av_ref.shape[0]
    piece = samples // len(order)
    share = piece // groups
    copies = []
    for g in range(groups):
        for n, j in enumerate(order):
            source = pl.ds((me ^ j) * piece + g * share, share)
            place = (g * len(order) + n) * share
            at = g * len(order) + n
            pair = (
                pltpu.make_async_copy(av_hbm.at[source], av_ref.at[pl.ds(place, share)], av_sem.at[at]),
                pltpu.make_async_copy(up_hbm.at[source], up_ref.at[pl.ds(place, share)], up_sem.at[at]),
            )
            pair[0].start()
            pair[1].start()
            copies.append(pair)
    first = len(order)
    for pair in copies[:first]:
        pair[0].wait()
        pair[1].wait()
    width_sums(comp_t_ref, proj_ref, av_ref, up_ref, range(first * share), (send_ref, keep_ref))
    for pair in copies[first:]:
        pair[0].wait()
        pair[1].wait()


def sums_kernel(places, av_ref, up_ref, comp_t_ref, proj_ref, send_ref, keep_ref):
    width_sums(comp_t_ref, proj_ref, av_ref, up_ref, places, (send_ref, keep_ref))


def load_and_sum(order, groups, av, up, comp_t, proj):
    samples, width, features = av.shape
    rank = comp_t.shape[0]
    half = jax.ShapeDtypeStruct((samples // groups // 2, 2 * rank, features), F32)
    hbm = pl.BlockSpec(memory_space=pltpu.HBM)
    count = groups * len(order)
    return pl.pallas_call(
        functools.partial(load_kernel, order, groups),
        in_specs=[hbm, hbm, VMEM, VMEM],
        out_specs=[VMEM] * 4,
        out_shape=[half, half, jax.ShapeDtypeStruct(av.shape, BF16), jax.ShapeDtypeStruct(up.shape, BF16)],
        scratch_shapes=[pltpu.SemaphoreType.DMA((count,)), pltpu.SemaphoreType.DMA((count,))],
        compiler_params=pltpu.CompilerParams(vmem_limit_bytes=LOAD_LIMIT),
        cost_estimate=cost(2 * 3 * samples // groups * width * features * rank, 4 * av.size),
        name="load_and_sum",
    )(av, up, comp_t, proj)


def sum_group(places, av, up, comp_t, proj):
    samples, width, features = av.shape
    rank = comp_t.shape[0]
    half = jax.ShapeDtypeStruct((len(places) // 2, 2 * rank, features), F32)
    return pl.pallas_call(
        functools.partial(sums_kernel, places),
        in_specs=[VMEM] * 4,
        out_specs=[VMEM] * 2,
        out_shape=[half, half],
        compiler_params=pltpu.CompilerParams(vmem_limit_bytes=LIMIT),
        cost_estimate=cost(2 * 3 * len(places) * width * features * rank, 8 * half.size),
        name="sum_group",
    )(av, up, comp_t, proj)


def layer_back_kernel(keep_ref, got_ref, pair_ref):
    rank = keep_ref.shape[1] // 2
    for b in range(keep_ref.shape[0]):
        total = keep_ref[b] + got_ref[b].astype(F32)
        centred, grads = total[:rank], total[rank:]
        inverse = 1.0 / jnp.sqrt(jnp.mean(centred * centred, axis=0, keepdims=True) + 1e-05)
        normed = centred * inverse
        moment = jnp.mean(grads * normed, axis=0, keepdims=True)
        pair_ref[b] = (inverse * (grads - normed * moment)).astype(BF16)


def layer_back(keep, got):
    samples, twice, features = keep.shape
    return pl.pallas_call(
        layer_back_kernel,
        in_specs=[VMEM] * 2,
        out_specs=VMEM,
        out_shape=jax.ShapeDtypeStruct((samples, twice // 2, features), BF16),
        compiler_params=pltpu.CompilerParams(vmem_limit_bytes=LIMIT),
        cost_estimate=cost(16 * keep.size, 8 * keep.size),
        name="layer_back",
    )(keep, got)


def table_kernel(jobs, owners, chained, pairs, has_total, *refs):
    av_ref, up_ref, comp_t_ref, mix_ref, owner_ref, slot_ref = refs[:6]
    pair_refs, refs = refs[6:6 + pairs], refs[6 + pairs:]
    if has_total:
        total_ref, refs = refs[0], refs[1:]
    outs, (masked, onehot) = refs[:-2], refs[-2:]
    _, width, features = av_ref.shape
    me, here = lax.axis_index("dim"), lax.axis_index("dp")
    slots = lax.broadcasted_iota(jnp.int32, (SHARD, features), 0)
    comp_t = comp_t_ref[...]
    for n, (place, j, offset, piece, pair, at) in enumerate(jobs):
        back = pair_refs[pair][at]
        up = up_ref[place]
        both = dot_nt(av_ref[place], jnp.concatenate([comp_t, back])).astype(BF16)
        grad = up.astype(F32) + dot_nt(up, mix_ref[...])
        grad = (grad + dot_nn(both, jnp.concatenate([back, comp_t]))).astype(BF16)
        lookups = pl.ds(pl.multiple_of(((me ^ j) * piece + offset) * features, features), features)
        owner = owner_ref[:, lookups] ^ here
        columns = slice(n * features, (n + 1) * features)
        for o in range(owners):
            mask = jnp.where(owner == o, 1.0, 0.0).astype(BF16)
            masked[o * width:(o + 1) * width, columns] = grad * mask
        hit = slots == slot_ref[:, lookups]
        onehot[:, columns] = jnp.where(hit, 1.0, 0.0).astype(BF16)
    added = dot_nt(masked[...], onehot[...])
    if has_total:
        added = added + total_ref[...]
    if chained is None:
        outs[0][...] = added
        return
    part = width // len(chained)
    for c, chain in enumerate(chained):
        for n, o in enumerate(halves(chain[1:])):
            at = (o ^ chain[0]) * width + c * part
            outs[2 * c][n] = added[at:at + part].astype(BF16)
            at = o * width + c * part
            outs[2 * c + 1][n] = added[at:at + part]


def table_part(jobs, owners, chained, av, up, comp_t, mix, owner, slot, pairs, total):
    _, width, features = av.shape
    rank = comp_t.shape[0]
    if chained is None:
        shapes = [jax.ShapeDtypeStruct((owners * width, SHARD), F32)]
    else:
        part = (owners // 2, width // len(chained), SHARD)
        shapes = [jax.ShapeDtypeStruct(part, t) for _ in chained for t in (BF16, F32)]
    args = [av, up, comp_t, mix, owner, slot, *pairs] + ([] if total is None else [total])
    lookups = len(jobs) * features
    return pl.pallas_call(
        functools.partial(table_kernel, jobs, owners, chained, len(pairs), total is not None),
        in_specs=[VMEM] * len(args),
        out_specs=[VMEM] * len(shapes),
        out_shape=shapes,
        scratch_shapes=[
            pltpu.VMEM((owners * width, lookups), BF16),
            pltpu.VMEM((SHARD, lookups), BF16),
        ],
        compiler_params=pltpu.CompilerParams(vmem_limit_bytes=LIMIT),
        cost_estimate=cost(
            2 * lookups * width * (features + 4 * rank + owners * SHARD),
            2 * lookups * width * owners,
        ),
        name="table_part",
    )(*args)


def finish_kernel(*refs):
    *ins, out_ref = refs
    part = out_ref.shape[0] // (len(ins) // 2)
    for c in range(len(ins) // 2):
        out_ref[c * part:(c + 1) * part] = ins[2 * c][0] + ins[2 * c + 1][0].astype(F32)


def finish(sums, width):
    args = [a for pair in sums for a in pair]
    return pl.pallas_call(
        finish_kernel,
        in_specs=[VMEM] * len(args),
        out_specs=VMEM,
        out_shape=jax.ShapeDtypeStruct((width, SHARD), F32),
        compiler_params=pltpu.CompilerParams(vmem_limit_bytes=LIMIT),
        name="finish",
    )(*args)


def swap(x, axis, bit):
    return lax.ppermute(x, axis, [(i, i ^ bit) for i in range(lax.axis_size(axis))])


def shards(attribute_vectors, upstream, compress, interact_proj, linear_mix, row_owner, row_slot):
    owners, peers = lax.axis_size("dp"), lax.axis_size("dim")
    samples, width, features = attribute_vectors.shape
    piece = samples // peers
    groups = min(2, piece)
    share = piece // groups
    comp_t = compress.T

    bits = bits_of(peers)
    held = halves(bits)
    order = held[peers // 2:] + held[:peers // 2]
    place_of = {j: n for n, j in enumerate(order)}

    send, keep, av, up = load_and_sum(order, groups, attribute_vectors, upstream, comp_t, interact_proj)
    parts = [(send, keep)]
    for g in range(1, groups):
        places = range(g * peers * share, (g + 1) * peers * share)
        parts.append(sum_group(places, av, up, comp_t, interact_proj))

    total = None
    owner, slot = row_owner.reshape(1, -1), row_slot.reshape(1, -1)
    low = bits_of(owners)[:(owners.bit_length() - 1) // 2]
    high = bits_of(owners)[len(low):]
    chains = [low + high, high[:1] + low + high[1:]]
    for g, (send, keep) in enumerate(parts):
        got = swap(send, "dim", bits[0])
        for bit in bits[1:]:
            keep = keep + got.astype(F32)
            half = keep.shape[0] // 2
            got = swap(keep[half:].astype(BF16), "dim", bit)
            keep = keep[:half]
        pairs, have = [layer_back(keep, got)], [0]
        for bit in reversed(bits):
            pairs += [swap(pair, "dim", bit) for pair in pairs]
            have += [j ^ bit for j in have]
        jobs = []
        for at, j in enumerate(have):
            for s in range(share):
                jobs.append(((g * peers + place_of[j]) * share + s, j, g * share + s, piece, at, s))
        chained = chains if g == groups - 1 else None
        outs = table_part(
            jobs, owners, chained, av, up, comp_t, linear_mix, owner, slot, pairs, total
        )
        total = outs[0]

    sums = []
    for c, chain in enumerate(chains):
        send, keep = outs[2 * c], outs[2 * c + 1]
        got = swap(send, "dp", chain[0])
        for bit in chain[1:]:
            keep = keep + got.astype(F32)
            half = keep.shape[0] // 2
            got = swap(keep[half:].astype(BF16), "dp", bit)
            keep = keep[:half]
        sums.append((keep, got))
    return finish(sums, width)


def solution(mesh):
    placed = (
        P("dp", "dim", None),
        P("dp", "dim", None),
        P(),
        P(None, "dim"),
        P(),
        P("dp", None),
        P("dp"),
    )
    return jax.shard_map(
        shards, mesh=mesh, in_specs=placed, out_specs=P("dim", "dp"), check_vma=False
    )
```

```python
import functools

import jax
import jax.numpy as jnp
from jax import lax
from jax.experimental import pallas as pl
from jax.experimental.pallas import tpu as pltpu
from jax.sharding import PartitionSpec as P

SHARD = 256
F32, BF16 = jnp.float32, jnp.bfloat16
LIMIT = 20 * 2**20
LOAD_LIMIT = 51 * 2**20
VMEM = pl.BlockSpec(memory_space=pltpu.VMEM)
HBM = pl.BlockSpec(memory_space=pltpu.HBM)


def dot_nt(a, b):
    return lax.dot_general(a, b, (((1,), (1,)), ((), ())), preferred_element_type=F32)


def dot_nn(a, b):
    return lax.dot_general(a, b, (((1,), (0,)), ((), ())), preferred_element_type=F32)


def bits_of(size):
    return [1 << t for t in range(size.bit_length() - 1)]


def halves(bits):
    numbers = [0]
    for bit in reversed(bits):
        numbers += [n ^ bit for n in numbers]
    return numbers


def call(kernel, name, args, shapes, flops, limit=LIMIT, specs=None, scratch=()):
    moved = sum(a.size * a.dtype.itemsize for a in (*args, *shapes))
    return pl.pallas_call(
        kernel,
        in_specs=specs or [VMEM] * len(args),
        out_specs=[VMEM] * len(shapes),
        out_shape=list(shapes),
        scratch_shapes=list(scratch),
        compiler_params=pltpu.CompilerParams(vmem_limit_bytes=limit),
        cost_estimate=pl.CostEstimate(flops=flops, bytes_accessed=moved, transcendentals=0),
        name=name,
    )(*args)


def width_sums(comp_t_ref, proj_ref, av_ref, up_ref, place, out_ref, at):
    rank = comp_t_ref.shape[0]
    reduced = dot_nt(comp_t_ref[...], av_ref[place]).astype(BF16)
    sums = dot_nn(reduced, av_ref[place])
    out_ref[at, :rank] = sums - jnp.mean(sums, axis=0, keepdims=True)
    grads = dot_nn(proj_ref[...], up_ref[place])
    out_ref[at, rank:] = grads - jnp.mean(grads, axis=0, keepdims=True)


def load_kernel(order, av_hbm, up_hbm, comp_hbm, proj_hbm, out_ref, av_ref, up_ref, comp_t_ref, proj_ref, sems):
    me = lax.axis_index("dim")
    piece = av_ref.shape[0] // len(order)
    copies = [
        pltpu.make_async_copy(comp_hbm, comp_t_ref, sems.at[0]),
        pltpu.make_async_copy(proj_hbm, proj_ref, sems.at[1]),
    ]
    for n, j in enumerate(order):
        source = pl.ds((me ^ j) * piece, piece)
        to = pl.ds(n * piece, piece)
        copies.append(pltpu.make_async_copy(av_hbm.at[source], av_ref.at[to], sems.at[2 + 2 * n]))
        copies.append(pltpu.make_async_copy(up_hbm.at[source], up_ref.at[to], sems.at[3 + 2 * n]))
    for copy in copies:
        copy.start()
    first = 2 + 2 * (len(order) // 4)
    for copy in copies[:first]:
        copy.wait()
    for at in range(out_ref.shape[0]):
        width_sums(comp_t_ref, proj_ref, av_ref, up_ref, at, out_ref, at)
    for copy in copies[first:]:
        copy.wait()


def sums_kernel(start, av_ref, up_ref, comp_t_ref, proj_ref, *out_refs):
    for out_ref in out_refs:
        for at in range(out_ref.shape[0]):
            width_sums(comp_t_ref, proj_ref, av_ref, up_ref, start + at, out_ref, at)
        start += out_ref.shape[0]


def prepare_kernel(start, av_ref, up_ref, comp_t_ref, proj_ref, mix_ref, slot_ref, out_ref, linear_ref, onehot_ref):
    sums_kernel(start, av_ref, up_ref, comp_t_ref, proj_ref, out_ref)
    samples, width, features = up_ref.shape
    for b in range(samples):
        up = up_ref[b]
        linear_ref[b] = up.astype(F32) + dot_nt(up, mix_ref[...])
    slots = lax.broadcasted_iota(jnp.int32, (SHARD, features), 0)
    for at in range(0, samples * features, features):
        hit = slots == slot_ref[:, at:at + features]
        onehot_ref[:, at:at + features] = jnp.where(hit, 1.0, 0.0).astype(BF16)


def layer_back_kernel(*refs):
    *terms, pair_ref = refs
    rank = pair_ref.shape[1]
    for b in range(pair_ref.shape[0]):
        total = sum(term[b].astype(F32) for term in terms)
        centred, grads = total[:rank], total[rank:]
        inverse = 1.0 / jnp.sqrt(jnp.mean(centred * centred, axis=0, keepdims=True) + 1e-05)
        normed = centred * inverse
        moment = jnp.mean(grads * normed, axis=0, keepdims=True)
        pair_ref[b] = (inverse * (grads - normed * moment)).astype(BF16)


def table_kernel(jobs, chains, last, pairs, has_total, *refs):
    av_ref, comp_t_ref, linear_ref, owner_ref, onehot_ref = refs[:5]
    pair_refs, refs = refs[5:5 + pairs], refs[5 + pairs:]
    if has_total:
        total_ref, refs = refs[0], refs[1:]
    outs, (masked, onehot) = refs[:-2], refs[-2:]
    _, width, features = av_ref.shape
    me, here = lax.axis_index("dim"), lax.axis_index("dp")
    odd = me % 2 == 1
    comp_t = comp_t_ref[...]
    ids = [here ^ jnp.where(odd, b, a) for a, b in zip(*[halves(chain) for chain in chains])]
    for n, (place, j, offset, piece, pair, at) in enumerate(jobs):
        back = pair_refs[pair][at]
        both = dot_nt(av_ref[place], jnp.concatenate([comp_t, back])).astype(BF16)
        grad = linear_ref[place] + dot_nn(both, jnp.concatenate([back, comp_t]))
        grad = grad.astype(BF16)
        lookups = pl.ds(pl.multiple_of(((me ^ j) * piece + offset) * features, features), features)
        owner = owner_ref[:, lookups]
        columns = slice(n * features, (n + 1) * features)
        for o, number in enumerate(ids):
            mask = jnp.where(owner == number, 1.0, 0.0).astype(BF16)
            masked[o * width:(o + 1) * width, columns] = grad * mask
        onehot[:, columns] = onehot_ref[:, lookups]
    added = dot_nt(masked[...], onehot[...])
    if has_total:
        added = added + total_ref[...]
    if not last:
        outs[0][...] = added
        return
    half = len(ids) // 2
    for n in range(half):
        outs[0][n] = added[(half + n) * width:(half + n + 1) * width].astype(BF16)
        outs[1][n] = added[n * width:(n + 1) * width]


def table_part(jobs, chains, last, av, comp_t, linear, owner, onehot, pairs, total):
    _, width, features = av.shape
    rank = comp_t.shape[0]
    owners = 1 << len(chains[0])
    if last:
        shapes = [jax.ShapeDtypeStruct((owners // 2, width, SHARD), t) for t in (BF16, F32)]
    else:
        shapes = [jax.ShapeDtypeStruct((owners * width, SHARD), F32)]
    args = [av, comp_t, linear, owner, onehot, *pairs] + ([] if total is None else [total])
    lookups = len(jobs) * features
    return call(
        functools.partial(table_kernel, jobs, chains, last, len(pairs), total is not None),
        "table_part",
        args,
        shapes,
        2 * lookups * width * (4 * rank + owners * SHARD),
        scratch=[pltpu.VMEM((owners * width, lookups), BF16), pltpu.VMEM((SHARD, lookups), BF16)],
    )


def finish_kernel(keep_ref, got_ref, out_ref):
    out_ref[...] = keep_ref[0] + got_ref[0].astype(F32)


def swap(x, bit):
    return lax.ppermute(x, "dim", [(i, i ^ bit) for i in range(lax.axis_size("dim"))])


def swap_rows(x, chains, step):
    owners, peers = lax.axis_size("dp"), lax.axis_size("dim")
    return lax.ppermute(
        x,
        ("dp", "dim"),
        [
            (a * peers + b, (a ^ chains[b % 2][step]) * peers + b)
            for a in range(owners)
            for b in range(peers)
        ],
    )


def shards(attribute_vectors, upstream, compress, interact_proj, linear_mix, row_owner, row_slot):
    owners, peers = lax.axis_size("dp"), lax.axis_size("dim")
    samples, width, features = attribute_vectors.shape
    rank = compress.shape[1]
    piece = samples // peers
    quarter = samples // 4
    shape = jax.ShapeDtypeStruct
    part = shape((quarter, 2 * rank, features), F32)
    sample_flops = 6 * width * features * rank

    bits = bits_of(peers)
    held = halves(bits)
    count = peers // 4
    order = held[3 * count:] + held[2 * count:3 * count] + held[count:2 * count] + held[:count]
    place_of = {j: n for n, j in enumerate(order)}

    send_high, av, up, comp_t, proj = call(
        functools.partial(load_kernel, order),
        "load_and_sum",
        (attribute_vectors, upstream, compress.T, interact_proj),
        [
            part,
            shape(upstream.shape, BF16),
            shape(upstream.shape, BF16),
            shape((rank, features), BF16),
            shape(interact_proj.shape, BF16),
        ],
        quarter * sample_flops,
        limit=LOAD_LIMIT,
        specs=[HBM] * 4,
        scratch=[pltpu.SemaphoreType.DMA((2 * peers + 2,))],
    )
    args = (av, up, comp_t, proj)
    got_high = swap(send_high, bits[0])
    send_low, keep_high = call(
        functools.partial(sums_kernel, quarter), "sums", args, [part] * 2, 2 * quarter * sample_flops
    )
    got_low = swap(send_low, bits[0])
    got = swap((keep_high + got_high).astype(BF16), bits[1])
    keep_low, linear, onehot = call(
        functools.partial(prepare_kernel, 3 * quarter),
        "prepare",
        (*args, linear_mix, row_slot.reshape(1, -1)),
        [part, shape(up.shape, F32), shape((SHARD, samples * features), BF16)],
        2 * samples * width * features * features,
    )
    terms = [keep_low, got_low, got]
    for bit in bits[2:]:
        keep = sum(term.astype(F32) for term in terms)
        half = keep.shape[0] // 2
        terms = [keep[:half], swap(keep[half:].astype(BF16), bit)]
    (pair,) = call(
        layer_back_kernel, "layer_back", terms, [shape((piece, rank, features), BF16)], 16 * terms[0].size
    )
    pairs, have = [pair], [0]
    for bit in reversed(bits):
        pairs += [swap(pair, bit) for pair in pairs]
        have += [j ^ bit for j in have]
    pairs = dict(zip(have, pairs))

    low = bits_of(owners)[:(owners.bit_length() - 1) // 2]
    high = bits_of(owners)[len(low):]
    chains = [low + high, high[:1] + low + high[1:]]
    stages = [[0, bits[0]]]
    for bit in reversed(bits[1:]):
        new = [j ^ bit for stage in stages for j in stage]
        stages += [[j for j in new if not j & bits[0]], [j for j in new if j & bits[0]]]
    total = None
    for stage in stages:
        jobs = [
            (place_of[j] * piece + s, j, s, piece, at, s)
            for at, j in enumerate(stage)
            for s in range(piece)
        ]
        outs = table_part(
            jobs, chains, stage is stages[-1], av, comp_t, linear, row_owner.reshape(1, -1), onehot,
            [pairs[j] for j in stage], total,
        )
        total = outs[0]

    send, keep = outs
    got = swap_rows(send, chains, 0)
    for step in range(1, len(chains[0])):
        keep = keep + got.astype(F32)
        half = keep.shape[0] // 2
        got = swap_rows(keep[half:].astype(BF16), chains, step)
        keep = keep[:half]
    (out,) = call(finish_kernel, "finish", (keep, got), [shape((width, SHARD), F32)], width * SHARD)
    return out


def solution(mesh):
    placed = (
        P("dp", "dim", None),
        P("dp", "dim", None),
        P(),
        P(None, "dim"),
        P(),
        P("dp", None),
        P("dp"),
    )
    return jax.shard_map(
        shards, mesh=mesh, in_specs=placed, out_specs=P("dim", "dp"), check_vma=False
    )
```

```python
import functools

import jax
import jax.numpy as jnp
from jax import lax
from jax.experimental import pallas as pl
from jax.experimental.pallas import tpu as pltpu
from jax.sharding import PartitionSpec as P

SHARD = 256
F32, BF16 = jnp.float32, jnp.bfloat16
LIMIT = 20 * 2**20
LOAD_LIMIT = 52600 * 2**10
VMEM = pl.BlockSpec(memory_space=pltpu.VMEM)
HBM = pl.BlockSpec(memory_space=pltpu.HBM)


def dot_nt(a, b):
    return lax.dot_general(a, b, (((1,), (1,)), ((), ())), preferred_element_type=F32)


def dot_nn(a, b):
    return lax.dot_general(a, b, (((1,), (0,)), ((), ())), preferred_element_type=F32)


def bits_of(size):
    return [1 << t for t in range(size.bit_length() - 1)]


def halves(bits):
    numbers = [0]
    for bit in reversed(bits):
        numbers += [n ^ bit for n in numbers]
    return numbers


def call(kernel, name, args, shapes, flops, limit=LIMIT, specs=None, scratch=()):
    moved = sum(a.size * a.dtype.itemsize for a in (*args, *shapes))
    return pl.pallas_call(
        kernel,
        in_specs=specs or [VMEM] * len(args),
        out_specs=[VMEM] * len(shapes),
        out_shape=list(shapes),
        scratch_shapes=list(scratch),
        compiler_params=pltpu.CompilerParams(vmem_limit_bytes=limit),
        cost_estimate=pl.CostEstimate(flops=flops, bytes_accessed=moved, transcendentals=0),
        name=name,
    )(*args)


def width_sums(comp_t_ref, proj_ref, av_ref, up_ref, place, out_ref, at):
    rank = comp_t_ref.shape[0]
    reduced = dot_nt(comp_t_ref[...], av_ref[place]).astype(BF16)
    sums = dot_nn(reduced, av_ref[place])
    out_ref[at, :rank] = sums - jnp.mean(sums, axis=0, keepdims=True)
    grads = dot_nn(proj_ref[...], up_ref[place])
    out_ref[at, rank:] = grads - jnp.mean(grads, axis=0, keepdims=True)


def load_kernel(order, av_hbm, up_hbm, av_ref, up_ref, sems):
    me = lax.axis_index("dim")
    piece = av_ref.shape[0] // len(order)
    copies = []
    for n, j in enumerate(order):
        source = pl.ds((me ^ j) * piece, piece)
        to = pl.ds(n * piece, piece)
        copies.append(pltpu.make_async_copy(av_hbm.at[source], av_ref.at[to], sems.at[2 * n]))
        copies.append(pltpu.make_async_copy(up_hbm.at[source], up_ref.at[to], sems.at[2 * n + 1]))
    for copy in copies:
        copy.start()
    for copy in copies:
        copy.wait()


def sums_kernel(start, av_ref, up_ref, comp_t_ref, proj_ref, *out_refs):
    for out_ref in out_refs:
        for at in range(out_ref.shape[0]):
            width_sums(comp_t_ref, proj_ref, av_ref, up_ref, start + at, out_ref, at)
        start += out_ref.shape[0]


def prepare_kernel(start, av_ref, up_ref, comp_t_ref, proj_ref, mix_ref, slot_ref, out_ref, linear_ref, onehot_ref):
    sums_kernel(start, av_ref, up_ref, comp_t_ref, proj_ref, out_ref)
    samples, width, features = up_ref.shape
    for b in range(samples):
        up = up_ref[b]
        linear_ref[b] = up.astype(F32) + dot_nt(up, mix_ref[...])
    slots = lax.broadcasted_iota(jnp.int32, (SHARD, features), 0)
    for at in range(0, samples * features, features):
        hit = slots == slot_ref[:, at:at + features]
        onehot_ref[:, at:at + features] = jnp.where(hit, 1.0, 0.0).astype(BF16)


def layer_back_kernel(*refs):
    *terms, pair_ref = refs
    rank = pair_ref.shape[1]
    for b in range(pair_ref.shape[0]):
        total = sum(term[b].astype(F32) for term in terms)
        centred, grads = total[:rank], total[rank:]
        inverse = 1.0 / jnp.sqrt(jnp.mean(centred * centred, axis=0, keepdims=True) + 1e-05)
        normed = centred * inverse
        moment = jnp.mean(grads * normed, axis=0, keepdims=True)
        pair_ref[b] = (inverse * (grads - normed * moment)).astype(BF16)


def add_lookups(grad, owner_ref, at, numbers, masked, columns):
    width, features = grad.shape
    owner = owner_ref[:, pl.ds(pl.multiple_of(at * features, features), features)]
    for o, number in enumerate(numbers):
        mask = jnp.where(owner == number, 1.0, 0.0).astype(BF16)
        masked[o * width:(o + 1) * width, columns] = grad * mask


def feature_grad(av, back, comp_t, linear):
    both = dot_nt(av, jnp.concatenate([comp_t, back])).astype(BF16)
    return (linear + dot_nn(both, jnp.concatenate([back, comp_t]))).astype(BF16)


def table_kernel(jobs, owners, last, pairs, has_total, *refs):
    av_ref, comp_t_ref, linear_ref, owner_ref, onehot_ref = refs[:5]
    pair_refs, refs = refs[5:5 + pairs], refs[5 + pairs:]
    if has_total:
        total_ref, refs = refs[0], refs[1:]
    outs, (masked, onehot) = refs[:-2], refs[-2:]
    _, width, features = av_ref.shape
    me, here = lax.axis_index("dim"), lax.axis_index("dp")
    comp_t = comp_t_ref[...]
    numbers = [here ^ m for m in owners]
    for n, (place, j, offset, piece, pair, at) in enumerate(jobs):
        grad = feature_grad(av_ref[place], pair_refs[pair][at], comp_t, linear_ref[place])
        at = (me ^ j) * piece + offset
        columns = slice(n * features, (n + 1) * features)
        add_lookups(grad, owner_ref, at, numbers, masked, columns)
        lookups = pl.ds(pl.multiple_of(at * features, features), features)
        onehot[:, columns] = onehot_ref[:, lookups]
    added = dot_nt(masked[...], onehot[...])
    if has_total:
        added = added + total_ref[...]
    if not last:
        outs[0][...] = added
        return
    half = width // len(last)
    for c, chain in enumerate(last):
        for n, o in enumerate(halves(chain[1:])):
            at = (o ^ chain[0]) * width + c * half
            outs[2 * c][n] = added[at:at + half].astype(BF16)
            at = o * width + c * half
            outs[2 * c + 1][n] = added[at:at + half]


def table_part(jobs, owners, last, av, comp_t, linear, owner, onehot, pairs, total):
    _, width, features = av.shape
    rank = comp_t.shape[0]
    shape = jax.ShapeDtypeStruct
    lookups = len(jobs) * features
    if last:
        part = (len(owners) // 2, width // len(last), SHARD)
        shapes = [shape(part, t) for _ in last for t in (BF16, F32)]
    else:
        shapes = [shape((len(owners) * width, SHARD), F32)]
    args = [av, comp_t, linear, owner, onehot, *pairs] + ([] if total is None else [total])
    return call(
        functools.partial(table_kernel, jobs, owners, last, len(pairs), total is not None),
        "table_part",
        args,
        shapes,
        2 * lookups * width * (4 * rank + len(owners) * SHARD),
        scratch=[pltpu.VMEM((len(owners) * width, lookups), BF16), pltpu.VMEM((SHARD, lookups), BF16)],
    )


def fold_kernel(*refs):
    *terms, send_ref, keep_ref = refs
    half = keep_ref.shape[0]
    start = 0
    for keep, got in zip(terms[::2], terms[1::2]):
        stop = start + keep.shape[1]
        send_ref[:, start:stop] = (keep[half:] + got[half:].astype(F32)).astype(BF16)
        keep_ref[:, start:stop] = keep[:half] + got[:half].astype(F32)
        start = stop


def fold(terms):
    count, _, slots = terms[0].shape
    part = (count // 2, sum(keep.shape[1] for keep in terms[::2]), slots)
    shapes = [jax.ShapeDtypeStruct(part, t) for t in (BF16, F32)]
    return call(fold_kernel, "fold", terms, shapes, terms[0].size)


def finish_kernel(*refs):
    *terms, out_ref = refs
    start = 0
    for keep, got in zip(terms[::2], terms[1::2]):
        stop = start + keep.shape[1]
        out_ref[start:stop] = keep[0] + got[0].astype(F32)
        start = stop


def swap(x, bit, axis="dim"):
    return lax.ppermute(x, axis, [(i, i ^ bit) for i in range(lax.axis_size(axis))])


def shards(attribute_vectors, upstream, compress, interact_proj, linear_mix, row_owner, row_slot):
    owners, peers = lax.axis_size("dp"), lax.axis_size("dim")
    samples, width, features = attribute_vectors.shape
    rank = compress.shape[1]
    piece = samples // peers
    quarter = samples // 4
    shape = jax.ShapeDtypeStruct
    part = shape((quarter, 2 * rank, features), F32)
    sample_flops = 6 * width * features * rank

    bits = bits_of(peers)
    held = halves(bits)
    count = peers // 4
    order = held[3 * count:] + held[2 * count:3 * count] + held[count:2 * count] + held[:count]
    place_of = {j: n for n, j in enumerate(order)}

    av, up = call(
        functools.partial(load_kernel, order),
        "load",
        (attribute_vectors, upstream),
        [shape(upstream.shape, BF16)] * 2,
        0,
        limit=LOAD_LIMIT,
        specs=[HBM] * 2,
        scratch=[pltpu.SemaphoreType.DMA((2 * peers,))],
    )
    comp_t = compress.T
    args = (av, up, comp_t, interact_proj)
    (send_high,) = call(
        functools.partial(sums_kernel, 0), "sums", args, [part], quarter * sample_flops
    )
    got_high = swap(send_high, bits[0])
    send_low, keep_high = call(
        functools.partial(sums_kernel, quarter), "sums", args, [part] * 2, 2 * quarter * sample_flops
    )
    got_low = swap(send_low, bits[0])
    got = swap((keep_high + got_high).astype(BF16), bits[1])
    keep_low, linear, onehot = call(
        functools.partial(prepare_kernel, 3 * quarter),
        "prepare",
        (*args, linear_mix, row_slot.reshape(1, -1)),
        [part, shape(up.shape, F32), shape((SHARD, samples * features), BF16)],
        2 * samples * width * features * features,
    )
    terms = [keep_low, got_low, got]
    for bit in bits[2:]:
        keep = sum(term.astype(F32) for term in terms)
        half = keep.shape[0] // 2
        terms = [keep[:half], swap(keep[half:].astype(BF16), bit)]
    (pair,) = call(
        layer_back_kernel, "layer_back", terms, [shape((piece, rank, features), BF16)], 16 * terms[0].size
    )
    owner = row_owner.reshape(1, -1)
    numbers = list(range(owners))

    def jobs_of(stage):
        return [
            (place_of[j] * piece + s, j, s, piece, at, s) for at, j in enumerate(stage) for s in range(piece)
        ]

    pairs = {0: pair}
    total = None
    for bit in reversed(bits[1:]):
        pairs.update({j ^ bit: swap(got, bit) for j, got in pairs.items()})
    stages = []
    for n, j in enumerate(list(pairs)):
        if n == 1:
            stage = list(stages[0])
            (total,) = table_part(
                jobs_of(stage), numbers, None, av, comp_t, linear, owner, onehot, [pairs[i] for i in stage], total
            )
            pairs[j], total = lax.optimization_barrier((pairs[j], total))
        pairs[j ^ bits[0]] = swap(pairs[j], bits[0])
        stages += [[j, j ^ bits[0]]] if n == 0 else [[j], [j ^ bits[0]]]
    for stage in stages[1:-1]:
        (total,) = table_part(
            jobs_of(stage), numbers, None, av, comp_t, linear, owner, onehot, [pairs[j] for j in stage], total
        )
    stage = stages[-1]
    low = bits_of(owners)[:(owners.bit_length() - 1) // 2]
    high = bits_of(owners)[len(low):]
    chains = [low + high, high[:1] + low + high[1:]]
    outs = table_part(
        jobs_of(stage), numbers, chains, av, comp_t, linear, owner, onehot, [pairs[j] for j in stage], total
    )
    sums = []
    for chain, send, keep in zip(chains, outs[::2], outs[1::2]):
        got = swap(send, chain[0], "dp")
        for bit in chain[1:len(low) + 1]:
            send, keep = fold([keep, got])
            got = swap(send, bit, "dp")
        sums += [keep, got]
    for bit in high[1:]:
        send, keep = fold(sums)
        sums = [keep, swap(send, bit, "dp")]
    (out,) = call(finish_kernel, "finish", sums, [shape((width, SHARD), F32)], width * SHARD)
    return out


def solution(mesh):
    placed = (
        P("dp", "dim", None),
        P("dp", "dim", None),
        P(),
        P(None, "dim"),
        P(),
        P("dp", None),
        P("dp"),
    )
    return jax.shard_map(
        shards, mesh=mesh, in_specs=placed, out_specs=P("dim", "dp"), check_vma=False
    )
```

```python
import functools

import jax
import jax.numpy as jnp
from jax import lax
from jax.experimental import pallas as pl
from jax.experimental.pallas import tpu as pltpu
from jax.sharding import PartitionSpec as P

SHARD = 256
F32, BF16 = jnp.float32, jnp.bfloat16
LIMIT = 20 * 2**20
LOAD_LIMIT = 52600 * 2**10
VMEM = pl.BlockSpec(memory_space=pltpu.VMEM)
HBM = pl.BlockSpec(memory_space=pltpu.HBM)
shape = jax.ShapeDtypeStruct


def dot_nt(a, b):
    return lax.dot_general(a, b, (((1,), (1,)), ((), ())), preferred_element_type=F32)


def dot_nn(a, b):
    return lax.dot_general(a, b, (((1,), (0,)), ((), ())), preferred_element_type=F32)


def bits_of(size):
    return [1 << t for t in range(size.bit_length() - 1)]


def halves(bits):
    numbers = [0]
    for bit in reversed(bits):
        numbers += [n ^ bit for n in numbers]
    return numbers


def call(kernel, name, args, shapes, flops, limit=LIMIT, specs=None, scratch=()):
    moved = sum(a.size * a.dtype.itemsize for a in (*args, *shapes)) if flops > 1 else 1
    return pl.pallas_call(
        kernel,
        in_specs=specs or [VMEM] * len(args),
        out_specs=[VMEM] * len(shapes),
        out_shape=list(shapes),
        scratch_shapes=list(scratch),
        compiler_params=pltpu.CompilerParams(vmem_limit_bytes=limit),
        cost_estimate=pl.CostEstimate(flops=flops, bytes_accessed=moved, transcendentals=0),
        name=name,
    )(*args)


def load_kernel(order, piece, av_hbm, up_hbm, av_ref, up_ref, sems):
    me = lax.axis_index("dim")
    copies = []
    for n, j in enumerate(order):
        for s in range(piece):
            at = n * piece + s
            source = (me ^ j) * piece + s
            copies.append(pltpu.make_async_copy(av_hbm.at[source], av_ref.at[at], sems.at[2 * at]))
            copies.append(pltpu.make_async_copy(up_hbm.at[source], up_ref.at[at], sems.at[2 * at + 1]))
    for copy in copies:
        copy.start()
    for copy in copies:
        copy.wait()


def width_sums(comp_t_ref, proj_ref, av, up, out_ref, at):
    rank = comp_t_ref.shape[0]
    reduced = dot_nt(comp_t_ref[...], av).astype(BF16)
    sums = dot_nn(reduced, av)
    out_ref[at, :rank] = sums - jnp.mean(sums, axis=0, keepdims=True)
    grads = dot_nn(proj_ref[...], up)
    out_ref[at, rank:] = grads - jnp.mean(grads, axis=0, keepdims=True)


def sums_kernel(start, av_ref, up_ref, comp_t_ref, proj_ref, *out_refs):
    for out_ref in out_refs:
        for at in range(out_ref.shape[0]):
            width_sums(comp_t_ref, proj_ref, av_ref[start + at], up_ref[start + at], out_ref, at)
        start += out_ref.shape[0]


def prepare_kernel(
    order, piece, start, av_ref, up_ref, comp_t_ref, proj_ref, mix_ref, slot_ref, out_ref, linear_ref, onehot_ref
):
    sums_kernel(start, av_ref, up_ref, comp_t_ref, proj_ref, out_ref)
    me = lax.axis_index("dim")
    features = up_ref.shape[2]
    slots = lax.broadcasted_iota(jnp.int32, (SHARD, features), 0)
    for n, j in enumerate(order):
        for s in range(piece):
            at = n * piece + s
            up = up_ref[at]
            linear_ref[at] = up.astype(F32) + dot_nt(up, mix_ref[...])
            hit = slots == slot_ref[:, lookups_of(me, j, piece, s, features)]
            onehot_ref[:, at * features:(at + 1) * features] = jnp.where(hit, 1.0, 0.0).astype(BF16)


def lookups_of(me, j, piece, s, features):
    return pl.ds(pl.multiple_of(((me ^ j) * piece + s) * features, features), features)


def add_kernel(keep_ref, got_ref, *out_refs):
    start = 0
    for out_ref in out_refs:
        stop = start + out_ref.shape[0]
        out_ref[...] = (keep_ref[start:stop] + got_ref[start:stop]).astype(out_ref.dtype)
        start = stop


def layer_back_kernel(starts, *refs):
    *terms, pair_ref = refs
    rank = pair_ref.shape[1]
    for b in range(pair_ref.shape[0]):
        total = sum(term[start + b].astype(F32) for start, term in zip(starts, terms))
        centred, grads = total[:rank], total[rank:]
        inverse = 1.0 / jnp.sqrt(jnp.mean(centred * centred, axis=0, keepdims=True) + 1e-05)
        normed = centred * inverse
        moment = jnp.mean(grads * normed, axis=0, keepdims=True)
        pair_ref[b] = (inverse * (grads - normed * moment)).astype(BF16)


def table_kernel(jobs, piece, rows, chain, has_total, *refs):
    av_ref, comp_t_ref, linear_ref, owner_ref, onehot_ref = refs[:5]
    pair_refs, refs = refs[5:5 + len(jobs)], refs[5 + len(jobs):]
    if has_total:
        total_ref, refs = refs[0], refs[1:]
    *outs, masked = refs
    _, width, features = av_ref.shape
    me, here = lax.axis_index("dim"), lax.axis_index("dp")
    comp_t = comp_t_ref[...]
    count = rows[1] - rows[0]
    owners = masked.shape[0] // count
    share = pair_refs[0].shape[0]
    added = None
    for (j, place, offset), pair_ref in zip(jobs, pair_refs):
        for s in range(share):
            at = place + s
            back = pair_ref[s]
            both = dot_nt(av_ref[at, rows[0]:rows[1]], jnp.concatenate([comp_t, back])).astype(BF16)
            grad = linear_ref[at, rows[0]:rows[1]] + dot_nn(both, jnp.concatenate([back, comp_t]))
            grad = grad.astype(BF16)
            owner = owner_ref[:, lookups_of(me, j, piece, offset + s, features)] ^ here
            for o in range(owners):
                mask = jnp.where(owner == o, 1.0, 0.0).astype(BF16)
                masked[o * count:(o + 1) * count, s * features:(s + 1) * features] = grad * mask
        part = dot_nt(masked[...], onehot_ref[:, place * features:(place + share) * features])
        added = part if added is None else added + part
    if chain is None:
        outs[0][...] = added + total_ref[...] if has_total else added
        return

    def block(o):
        own = added[o * count:(o + 1) * count]
        return own + total_ref[o * width + rows[0]:o * width + rows[1]] if has_total else own

    for n, o in enumerate(halves(chain[1:])):
        outs[0][n] = block(o ^ chain[0]).astype(BF16)
        outs[1][n] = block(o)


def table_part(jobs, piece, rows, owners, chain, arrays, pairs, total):
    _, width, features = arrays[0].shape
    rank = arrays[1].shape[0]
    count = rows[1] - rows[0]
    share = pairs[0].shape[0]
    if chain is None:
        shapes = [shape((owners * width, SHARD), F32)]
    else:
        shapes = [shape((owners // 2, count, SHARD), t) for t in (BF16, F32)]
    return call(
        functools.partial(table_kernel, jobs, piece, rows, chain, total is not None),
        "table_part",
        [*arrays, *pairs] + ([] if total is None else [total]),
        shapes,
        1,
        scratch=[pltpu.VMEM((owners * count, share * features), BF16)],
    )


def fold_kernel(*refs):
    *terms, send_ref, keep_ref = refs
    half = keep_ref.shape[0]
    start = 0
    for keep, got in zip(terms[::2], terms[1::2]):
        stop = start + keep.shape[1]
        send_ref[:, start:stop] = (keep[half:] + got[half:].astype(F32)).astype(BF16)
        keep_ref[:, start:stop] = keep[:half] + got[:half].astype(F32)
        start = stop


def fold(terms):
    count, _, slots = terms[0].shape
    part = (count // 2, sum(keep.shape[1] for keep in terms[::2]), slots)
    return call(fold_kernel, "fold", terms, [shape(part, t) for t in (BF16, F32)], terms[0].size)


def finish_kernel(*refs):
    *terms, out_ref = refs
    start = 0
    for keep, got in zip(terms[::2], terms[1::2]):
        stop = start + keep.shape[1]
        out_ref[start:stop] = keep[0] + got[0].astype(F32)
        start = stop


def swap(x, bit, axis="dim"):
    return lax.ppermute(x, axis, [(i, i ^ bit) for i in range(lax.axis_size(axis))])


def after(x, *others):
    return lax.optimization_barrier((x, *others))[0]


def shards(attribute_vectors, upstream, compress, interact_proj, linear_mix, row_owner, row_slot):
    owners, peers = lax.axis_size("dp"), lax.axis_size("dim")
    samples, width, features = attribute_vectors.shape
    rank = compress.shape[1]
    piece = samples // peers
    quarter = samples // 4
    groups = 2 if peers == 4 else 1
    share = piece // groups
    sample_flops = 6 * width * features * rank

    bits = bits_of(peers)
    held = halves(bits)
    count = peers // 4
    order = held[3 * count:] + held[2 * count:3 * count] + held[count:2 * count] + held[:count]
    place_of = {j: n * piece for n, j in enumerate(order)}

    comp_t = compress.T
    owner, slot = row_owner.reshape(1, -1), row_slot.reshape(1, -1)
    part = shape((quarter, 2 * rank, features), F32)

    av, up = call(
        functools.partial(load_kernel, order, piece),
        "load",
        (attribute_vectors, upstream),
        [shape(upstream.shape, BF16)] * 2,
        0,
        limit=LOAD_LIMIT,
        specs=[HBM] * 2,
        scratch=[pltpu.SemaphoreType.DMA((2 * samples,))],
    )
    args = (av, up, comp_t, interact_proj)
    (send_high,) = call(
        functools.partial(sums_kernel, 0), "sums", args, [part], quarter * sample_flops
    )
    got_high = swap(send_high, bits[0])
    send_low, keep_high = call(
        functools.partial(sums_kernel, quarter), "sums", args, [part] * 2, 2 * quarter * sample_flops
    )
    got_low = swap(send_low, bits[0])
    sent = call(
        add_kernel,
        "add",
        (keep_high, got_high),
        [shape((quarter // groups, 2 * rank, features), BF16)] * groups,
        keep_high.size,
    )
    got = [swap(x, bits[1]) for x in sent]
    keep_low, linear, onehot = call(
        functools.partial(prepare_kernel, order, piece, 3 * quarter),
        "prepare",
        (*args, linear_mix, slot),
        [part, shape((samples, width, features), F32), shape((SHARD, samples * features), BF16)],
        2 * samples * width * features * features,
    )
    arrays = (av, comp_t, linear, owner, onehot)

    def layer_back(terms, starts):
        return call(
            functools.partial(layer_back_kernel, starts),
            "layer_back",
            terms,
            [shape((share, rank, features), BF16)],
            32 * share * rank * features,
        )[0]

    def table(total, *stage, rows=(0, width), chain=None):
        jobs = [(j, place_of[j] + g * share, g * share) for g, j in stage]
        outs = table_part(jobs, piece, rows, owners, chain, arrays, [pairs[g][j] for g, j in stage], total)
        return outs if chain else outs[0]

    pairs = [{} for _ in range(groups)]
    total = None
    if groups == 2:
        core, y = bits
        far = core ^ y
        pairs[0][0] = layer_back([keep_low, got_low, got[0]], [0, 0, 0])
        pairs[0][y] = swap(pairs[0][0], y)
        pairs[1][0] = layer_back([keep_low, got_low, after(got[1], pairs[0][0])], [share, share, 0])
        pairs[1][y] = swap(pairs[1][0], y)
        pairs[0][y] = after(pairs[0][y], pairs[1][0])
        pairs[0][core] = swap(after(pairs[0][0], pairs[0][y]), core)
        pairs[0][far] = swap(pairs[0][y], core)
        total = table(total, (0, 0), (0, y), (0, core), (0, far))
        pairs[1][y] = after(pairs[1][y], total)
        pairs[1][core] = swap(after(pairs[1][0], pairs[1][y]), core)
        pairs[1][far] = swap(pairs[1][y], core)
        total = table(total, (1, 0), (1, y))
        last = [(1, core), (1, far)]
    else:
        terms, starts = [keep_low, got_low, got[0]], [0, 0, 0]
        for bit in bits[2:]:
            keep = sum(term.astype(F32) for term in terms)
            half = keep.shape[0] // 2
            terms, starts = [keep[:half], swap(keep[half:].astype(BF16), bit)], [0, 0]
        pairs[0][0] = layer_back(terms, starts)
        for bit in reversed(bits):
            pairs[0].update({j ^ bit: swap(pair, bit) for j, pair in pairs[0].items()})
        *stage, last = [(0, j) for j in pairs[0]]
        for job in stage:
            total = table(total, job)
        last = [last]

    low = bits_of(owners)[:(owners.bit_length() - 1) // 2]
    high = bits_of(owners)[len(low):]
    chains = [low + high, high[:1] + low + high[1:]]
    sums = []
    for c, chain in enumerate(chains):
        rows = (c * width // 2, (c + 1) * width // 2)
        send, keep = table(total, *last, rows=rows, chain=chain)
        sums.append([keep, swap(send, chain[0], "dp")])
    for step in range(1, len(low) + 1):
        for c, chain in enumerate(chains):
            send, keep = fold(sums[c])
            sums[c] = [keep, swap(send, chain[step], "dp")]
    sums = sums[0] + sums[1]
    for bit in high[1:]:
        send, keep = fold(sums)
        sums = [keep, swap(send, bit, "dp")]
    (out,) = call(finish_kernel, "finish", sums, [shape((width, SHARD), F32)], width * SHARD)
    return out


def solution(mesh):
    placed = (
        P("dp", "dim", None),
        P("dp", "dim", None),
        P(),
        P(None, "dim"),
        P(),
        P("dp", None),
        P("dp"),
    )
    return jax.shard_map(
        shards, mesh=mesh, in_specs=placed, out_specs=P("dim", "dp"), check_vma=False
    )
```

```python
import functools

import jax
import jax.numpy as jnp
from jax import lax
from jax.experimental import pallas as pl
from jax.experimental.pallas import tpu as pltpu
from jax.sharding import PartitionSpec as P

SHARD = 256
F32, BF16 = jnp.float32, jnp.bfloat16
LIMIT = 20 * 2**20
LOAD_LIMIT = 52600 * 2**10
VMEM = pl.BlockSpec(memory_space=pltpu.VMEM)
HBM = pl.BlockSpec(memory_space=pltpu.HBM)
shape = jax.ShapeDtypeStruct


def dot_nt(a, b):
    return lax.dot_general(a, b, (((1,), (1,)), ((), ())), preferred_element_type=F32)


def dot_nn(a, b):
    return lax.dot_general(a, b, (((1,), (0,)), ((), ())), preferred_element_type=F32)


def bits_of(size):
    return [1 << t for t in range(size.bit_length() - 1)]


def halves(bits):
    numbers = [0]
    for bit in reversed(bits):
        numbers += [n ^ bit for n in numbers]
    return numbers


def call(kernel, name, args, shapes, flops, limit=LIMIT, specs=None, scratch=()):
    moved = sum(a.size * a.dtype.itemsize for a in (*args, *shapes))
    return pl.pallas_call(
        kernel,
        in_specs=specs or [VMEM] * len(args),
        out_specs=[VMEM] * len(shapes),
        out_shape=list(shapes),
        scratch_shapes=list(scratch),
        compiler_params=pltpu.CompilerParams(vmem_limit_bytes=limit),
        cost_estimate=pl.CostEstimate(flops=flops, bytes_accessed=moved, transcendentals=0),
        name=name,
    )(*args)


def load_kernel(piece, av_hbm, up_hbm, av_ref, up_ref, sems):
    me = lax.axis_index("dim")
    copies = []
    for j in range(av_ref.shape[0] // piece):
        source, to = pl.ds((me ^ j) * piece, piece), pl.ds(j * piece, piece)
        copies.append(pltpu.make_async_copy(av_hbm.at[source], av_ref.at[to], sems.at[2 * j]))
        copies.append(pltpu.make_async_copy(up_hbm.at[source], up_ref.at[to], sems.at[2 * j + 1]))
    for copy in copies:
        copy.start()
    for copy in copies:
        copy.wait()


def width_sums(comp_t_ref, proj_ref, av, up, out_ref, at):
    rank = comp_t_ref.shape[0]
    reduced = dot_nt(comp_t_ref[...], av).astype(BF16)
    sums = dot_nn(reduced, av)
    out_ref[at, :rank] = sums - jnp.mean(sums, axis=0, keepdims=True)
    grads = dot_nn(proj_ref[...], up)
    out_ref[at, rank:] = grads - jnp.mean(grads, axis=0, keepdims=True)


def sums_kernel(orders, piece, av_ref, up_ref, comp_t_ref, proj_ref, *out_refs):
    for order, out_ref in zip(orders, out_refs):
        for n in range(len(order) * piece):
            at = order[n // piece] * piece + n % piece
            width_sums(comp_t_ref, proj_ref, av_ref[at], up_ref[at], out_ref, n)


def prepare_kernel(low, piece, av_ref, up_ref, comp_t_ref, proj_ref, mix_ref, slot_ref, out_ref, linear_ref, onehot_ref):
    sums_kernel([low], piece, av_ref, up_ref, comp_t_ref, proj_ref, out_ref)
    me = lax.axis_index("dim")
    samples, _, features = up_ref.shape
    slots = lax.broadcasted_iota(jnp.int32, (SHARD, features), 0)
    for at in range(samples):
        b = at ^ (me * piece)
        up = up_ref[at]
        linear_ref[at] = up.astype(F32) + dot_nt(up, mix_ref[...])
        hit = slots == slot_ref[:, pl.ds(pl.multiple_of(b * features, features), features)]
        onehot_ref[at * features:(at + 1) * features] = jnp.where(hit, 1.0, 0.0).T.astype(BF16)


def add_kernel(keep_ref, got_ref, out_ref):
    out_ref[...] = (keep_ref[...] + got_ref[...]).astype(out_ref.dtype)


def add(keep, got):
    return call(add_kernel, "add", (keep, got), [shape(keep.shape, BF16)], keep.size)[0]


def layer_back_kernel(*refs):
    *terms, pair_ref = refs
    rank = pair_ref.shape[1]
    for b in range(pair_ref.shape[0]):
        total = sum(term[b].astype(F32) for term in terms)
        centred, grads = total[:rank], total[rank:]
        inverse = 1.0 / jnp.sqrt(jnp.mean(centred * centred, axis=0, keepdims=True) + 1e-05)
        normed = centred * inverse
        moment = jnp.mean(grads * normed, axis=0, keepdims=True)
        pair_ref[b] = (inverse * (grads - normed * moment)).astype(BF16)


def table_kernel(start, piece, chains, count, has_total, *refs):
    av_ref, comp_t_ref, linear_ref, owner_ref, onehot_ref = refs[:5]
    pair_refs, refs = refs[5:5 + count], refs[5 + count:]
    if has_total:
        total_ref, refs = refs[0], refs[1:]
    *outs, masked = refs
    _, width, features = av_ref.shape
    me, here = lax.axis_index("dim"), lax.axis_index("dp")
    comp_t = comp_t_ref[...]
    owners = masked.shape[0] // width
    for n in range(count * piece):
        at = start + n
        b = at ^ (me * piece)
        back = pair_refs[n // piece][n % piece]
        both = dot_nt(av_ref[at], jnp.concatenate([comp_t, back])).astype(BF16)
        grad = linear_ref[at] + dot_nn(both, jnp.concatenate([back, comp_t]))
        grad = grad.astype(BF16)
        owner = owner_ref[:, pl.ds(pl.multiple_of(b * features, features), features)] ^ here
        for o in range(owners):
            mask = jnp.where(owner == o, 1.0, 0.0).astype(BF16)
            masked[o * width:(o + 1) * width, n * features:(n + 1) * features] = grad * mask
    added = dot_nn(masked[...], onehot_ref[start * features:(start + count * piece) * features])
    if has_total:
        added = added + total_ref[...]
    if chains is None:
        outs[0][...] = added
        return
    half = width // len(chains)
    for c, chain in enumerate(chains):
        for n, o in enumerate(halves(chain[1:])):
            at = (o ^ chain[0]) * width + c * half
            outs[2 * c][n] = added[at:at + half].astype(BF16)
            at = o * width + c * half
            outs[2 * c + 1][n] = added[at:at + half]


def table_part(j, piece, owners, chains, arrays, pairs, total):
    _, width, features = arrays[0].shape
    lookups = len(pairs) * piece * features
    if chains is None:
        shapes = [shape((owners * width, SHARD), F32)]
    else:
        part = (owners // 2, width // len(chains), SHARD)
        shapes = [shape(part, t) for _ in chains for t in (BF16, F32)]
    return call(
        functools.partial(table_kernel, j * piece, piece, chains, len(pairs), total is not None),
        "table_part",
        [*arrays, *pairs] + ([] if total is None else [total]),
        shapes,
        2 * lookups * width * owners * SHARD,
        scratch=[pltpu.VMEM((owners * width, lookups), BF16)],
    )


def fold_kernel(*refs):
    *terms, send_ref, keep_ref = refs
    half = keep_ref.shape[0]
    start = 0
    for keep, got in zip(terms[::2], terms[1::2]):
        stop = start + keep.shape[1]
        send_ref[:, start:stop] = (keep[half:] + got[half:].astype(F32)).astype(BF16)
        keep_ref[:, start:stop] = keep[:half] + got[:half].astype(F32)
        start = stop


def fold(terms):
    count, _, slots = terms[0].shape
    part = (count // 2, sum(keep.shape[1] for keep in terms[::2]), slots)
    return call(fold_kernel, "fold", terms, [shape(part, t) for t in (BF16, F32)], terms[0].size)


def finish_kernel(*refs):
    *terms, out_ref = refs
    start = 0
    for keep, got in zip(terms[::2], terms[1::2]):
        stop = start + keep.shape[1]
        out_ref[start:stop] = keep[0] + got[0].astype(F32)
        start = stop


def swap(x, bit, axis="dim"):
    return lax.ppermute(x, axis, [(i, i ^ bit) for i in range(lax.axis_size(axis))])


def after(x, *others):
    return lax.optimization_barrier((x, *others))[0]


def shards(attribute_vectors, upstream, compress, interact_proj, linear_mix, row_owner, row_slot):
    owners, peers = lax.axis_size("dp"), lax.axis_size("dim")
    samples, width, features = attribute_vectors.shape
    rank = compress.shape[1]
    piece = samples // peers
    quarter = samples // 4
    sample_flops = 6 * width * features * rank

    bits = bits_of(peers)
    core = bits[0]
    held = halves(bits)
    count = peers // 4
    low, high = held[:count], held[count:2 * count]

    owner, slot = row_owner.reshape(1, -1), row_slot.reshape(1, -1)
    part = shape((quarter, 2 * rank, features), F32)
    comp_t, proj = compress.T, interact_proj
    av, up = call(
        functools.partial(load_kernel, piece),
        "load",
        (attribute_vectors, upstream),
        [shape(upstream.shape, BF16)] * 2,
        0,
        limit=LOAD_LIMIT,
        specs=[HBM] * 2,
        scratch=[pltpu.SemaphoreType.DMA((2 * peers,))],
    )
    args = (av, up, comp_t, proj)
    (send_high,) = call(
        functools.partial(sums_kernel, [[j ^ core for j in high]], piece),
        "first_sums",
        args,
        [part],
        quarter * sample_flops,
    )
    got_high = swap(send_high, core)
    keep_high, send_low = call(
        functools.partial(sums_kernel, [high, [j ^ core for j in low]], piece),
        "sums",
        args,
        [part] * 2,
        2 * quarter * sample_flops,
    )
    got_low = swap(send_low, core)
    got = swap(add(keep_high, got_high), bits[1])
    keep_low, linear, onehot = call(
        functools.partial(prepare_kernel, low, piece),
        "prepare",
        (*args, linear_mix, slot),
        [part, shape(up.shape, F32), shape((samples * features, SHARD), BF16)],
        2 * samples * width * features * features,
    )
    arrays = (av, comp_t, linear, owner, onehot)

    terms = [keep_low, got_low, got]
    for bit in bits[2:]:
        keep = sum(term.astype(F32) for term in terms)
        half = keep.shape[0] // 2
        terms = [keep[:half], swap(keep[half:].astype(BF16), bit)]
    (pair,) = call(
        layer_back_kernel,
        "layer_back",
        terms,
        [shape((piece, rank, features), BF16)],
        32 * piece * rank * features,
    )

    low_bits = bits_of(owners)[:(owners.bit_length() - 1) // 2]
    high_bits = bits_of(owners)[len(low_bits):]
    chains = [low_bits + high_bits, high_bits[:1] + low_bits + high_bits[1:]]
    pairs = {0: pair}
    (total,) = table_part(0, piece, owners, None, arrays, [pair], None)
    for bit in reversed(bits[1:]):
        pairs.update({j ^ bit: swap(got, bit) for j, got in pairs.items()})
    for j in list(pairs):
        pairs[j] = after(pairs[j], total) if j else pair
        pairs[j ^ core] = swap(pairs[j], core)
    middle = [pairs[j] for j in range(1, peers - 1)]
    (total,) = table_part(1, piece, owners, None, arrays, middle, total)
    outs = table_part(peers - 1, piece, owners, chains, arrays, [pairs[peers - 1]], total)

    sums = [[outs[2 * c + 1], swap(outs[2 * c], chain[0], "dp")] for c, chain in enumerate(chains)]
    for step in range(1, len(low_bits) + 1):
        for c, chain in enumerate(chains):
            send, keep = fold(sums[c])
            sums[c] = [keep, swap(send, chain[step], "dp")]
    sums = sums[0] + sums[1]
    for bit in high_bits[1:]:
        send, keep = fold(sums)
        sums = [keep, swap(send, bit, "dp")]
    (out,) = call(finish_kernel, "finish", sums, [shape((width, SHARD), F32)], width * SHARD)
    return out


def solution(mesh):
    placed = (
        P("dp", "dim", None),
        P("dp", "dim", None),
        P(),
        P(None, "dim"),
        P(),
        P("dp", None),
        P("dp"),
    )
    return jax.shard_map(
        shards, mesh=mesh, in_specs=placed, out_specs=P("dim", "dp"), check_vma=False
    )
```

```python
import functools

import jax
import jax.numpy as jnp
from jax import lax
from jax.experimental import pallas as pl
from jax.experimental.pallas import tpu as pltpu
from jax.sharding import PartitionSpec as P

SHARD = 256
F32, BF16 = jnp.float32, jnp.bfloat16
LIMIT = 20 * 2**20
LOAD_LIMIT = 52600 * 2**10
VMEM = pl.BlockSpec(memory_space=pltpu.VMEM)
HBM = pl.BlockSpec(memory_space=pltpu.HBM)
shape = jax.ShapeDtypeStruct


def dot_nt(a, b):
    return lax.dot_general(a, b, (((1,), (1,)), ((), ())), preferred_element_type=F32)


def dot_nn(a, b):
    return lax.dot_general(a, b, (((1,), (0,)), ((), ())), preferred_element_type=F32)


def bits_of(size):
    return [1 << t for t in range(size.bit_length() - 1)]


def halves(bits):
    numbers = [0]
    for bit in reversed(bits):
        numbers += [n ^ bit for n in numbers]
    return numbers


def call(kernel, name, args, shapes, flops, limit=LIMIT, specs=None, scratch=()):
    moved = sum(a.size * a.dtype.itemsize for a in (*args, *shapes))
    return pl.pallas_call(
        kernel,
        in_specs=specs or [VMEM] * len(args),
        out_specs=[VMEM] * len(shapes),
        out_shape=list(shapes),
        scratch_shapes=list(scratch),
        compiler_params=pltpu.CompilerParams(vmem_limit_bytes=limit),
        cost_estimate=pl.CostEstimate(flops=flops, bytes_accessed=moved, transcendentals=0),
        name=name,
    )(*args)


def load_kernel(piece, av_hbm, up_hbm, av_ref, up_ref, sems):
    me = lax.axis_index("dim")
    copies = []
    for j in range(av_ref.shape[0] // piece):
        source, to = pl.ds((me ^ j) * piece, piece), pl.ds(j * piece, piece)
        copies.append(pltpu.make_async_copy(av_hbm.at[source], av_ref.at[to], sems.at[2 * j]))
        copies.append(pltpu.make_async_copy(up_hbm.at[source], up_ref.at[to], sems.at[2 * j + 1]))
    for copy in copies:
        copy.start()
    for copy in copies:
        copy.wait()


def width_sums(comp_t_ref, proj_ref, av, up, out_ref, at):
    kind = out_ref.dtype
    rank = comp_t_ref.shape[0]
    reduced = dot_nt(comp_t_ref[...], av).astype(BF16)
    sums = dot_nn(reduced, av)
    out_ref[at, :rank] = (sums - jnp.mean(sums, axis=0, keepdims=True)).astype(kind)
    grads = dot_nn(proj_ref[...], up)
    out_ref[at, rank:] = (grads - jnp.mean(grads, axis=0, keepdims=True)).astype(kind)


def sums_kernel(orders, piece, av_ref, up_ref, comp_t_ref, proj_ref, *out_refs):
    for order, out_ref in zip(orders, out_refs):
        for n in range(len(order) * piece):
            at = order[n // piece] * piece + n % piece
            width_sums(comp_t_ref, proj_ref, av_ref[at], up_ref[at], out_ref, n)


def prepare_kernel(low, piece, av_ref, up_ref, comp_t_ref, proj_ref, mix_ref, slot_ref, out_ref, linear_ref, onehot_ref):
    sums_kernel([low], piece, av_ref, up_ref, comp_t_ref, proj_ref, out_ref)
    me = lax.axis_index("dim")
    samples, _, features = up_ref.shape
    slots = lax.broadcasted_iota(jnp.int32, (SHARD, features), 0)
    for at in range(samples):
        b = at ^ (me * piece)
        up = up_ref[at]
        linear_ref[at] = up.astype(F32) + dot_nt(up, mix_ref[...])
        hit = slots == slot_ref[:, pl.ds(pl.multiple_of(b * features, features), features)]
        onehot_ref[at * features:(at + 1) * features] = jnp.where(hit, 1.0, 0.0).T.astype(BF16)


def add_kernel(keep_ref, got_ref, out_ref):
    out_ref[...] = (keep_ref[...] + got_ref[...].astype(F32)).astype(out_ref.dtype)


def add(keep, got):
    return call(add_kernel, "add", (keep, got), [shape(keep.shape, BF16)], keep.size)[0]


def layer_back_kernel(*refs):
    *terms, pair_ref = refs
    rank = pair_ref.shape[1]
    for b in range(pair_ref.shape[0]):
        total = sum(term[b].astype(F32) for term in terms)
        centred, grads = total[:rank], total[rank:]
        inverse = 1.0 / jnp.sqrt(jnp.mean(centred * centred, axis=0, keepdims=True) + 1e-05)
        normed = centred * inverse
        moment = jnp.mean(grads * normed, axis=0, keepdims=True)
        pair_ref[b] = (inverse * (grads - normed * moment)).astype(BF16)


def table_kernel(start, piece, last, count, has_total, *refs):
    av_ref, comp_t_ref, linear_ref, owner_ref, onehot_ref = refs[:5]
    pair_refs, refs = refs[5:5 + count], refs[5 + count:]
    if has_total:
        total_ref, refs = refs[0], refs[1:]
    *outs, masked = refs
    _, width, features = av_ref.shape
    me, here = lax.axis_index("dim"), lax.axis_index("dp")
    comp_t = comp_t_ref[...]
    owners = masked.shape[0] // width
    for n in range(count * piece):
        at = start + n
        b = at ^ (me * piece)
        back = pair_refs[n // piece][n % piece]
        both = dot_nt(av_ref[at], jnp.concatenate([comp_t, back])).astype(BF16)
        grad = linear_ref[at] + dot_nn(both, jnp.concatenate([back, comp_t]))
        grad = grad.astype(BF16)
        owner = owner_ref[:, pl.ds(pl.multiple_of(b * features, features), features)] ^ here
        for o in range(owners):
            mask = jnp.where(owner == o, 1.0, 0.0).astype(BF16)
            masked[o * width:(o + 1) * width, n * features:(n + 1) * features] = grad * mask
    added = dot_nn(masked[...], onehot_ref[start * features:(start + count * piece) * features])
    if has_total:
        added = added + total_ref[...]
    if not last:
        outs[0][...] = added
        return
    for m, out in enumerate(outs):
        out[...] = added[m * width:(m + 1) * width].astype(out.dtype)


def table_part(j, piece, owners, last, arrays, pairs, total):
    _, width, features = arrays[0].shape
    lookups = len(pairs) * piece * features
    if last:
        shapes = [shape((width, SHARD), F32 if m == 0 else BF16) for m in range(owners)]
    else:
        shapes = [shape((owners * width, SHARD), F32)]
    return call(
        functools.partial(table_kernel, j * piece, piece, last, len(pairs), total is not None),
        "table_part",
        [*arrays, *pairs] + ([] if total is None else [total]),
        shapes,
        2 * lookups * width * owners * SHARD,
        scratch=[pltpu.VMEM((owners * width, lookups), BF16)],
    )


def finish_kernel(*refs):
    *terms, out_ref = refs
    out_ref[...] = sum(term[...].astype(F32) for term in terms)


def swap(x, bit, axis="dim"):
    return lax.ppermute(x, axis, [(i, i ^ bit) for i in range(lax.axis_size(axis))])


def after(x, *others):
    return lax.optimization_barrier((x, *others))[0]


def shards(attribute_vectors, upstream, compress, interact_proj, linear_mix, row_owner, row_slot):
    owners, peers = lax.axis_size("dp"), lax.axis_size("dim")
    samples, width, features = attribute_vectors.shape
    rank = compress.shape[1]
    piece = samples // peers
    quarter = samples // 4
    sample_flops = 6 * width * features * rank

    bits = bits_of(peers)
    core = bits[0]
    held = halves(bits)
    count = peers // 4
    low, high = held[:count], held[count:2 * count]

    owner, slot = row_owner.reshape(1, -1), row_slot.reshape(1, -1)
    part = shape((quarter, 2 * rank, features), F32)
    comp_t, proj = compress.T, interact_proj
    av, up = call(
        functools.partial(load_kernel, piece),
        "load",
        (attribute_vectors, upstream),
        [shape(upstream.shape, BF16)] * 2,
        0,
        limit=LOAD_LIMIT,
        specs=[HBM] * 2,
        scratch=[pltpu.SemaphoreType.DMA((2 * peers,))],
    )
    args = (av, up, comp_t, proj)
    (send_high,) = call(
        functools.partial(sums_kernel, [[j ^ core for j in high]], piece),
        "first_sums",
        args,
        [shape(part.shape, BF16)],
        quarter * sample_flops,
    )
    got_high = swap(send_high, core)
    keep_high, send_low = call(
        functools.partial(sums_kernel, [high, [j ^ core for j in low]], piece),
        "sums",
        args,
        [part] * 2,
        2 * quarter * sample_flops,
    )
    got_low = swap(send_low, core)
    got = swap(add(keep_high, got_high), bits[1])
    keep_low, linear, onehot = call(
        functools.partial(prepare_kernel, low, piece),
        "prepare",
        (*args, linear_mix, slot),
        [part, shape(up.shape, F32), shape((samples * features, SHARD), BF16)],
        2 * samples * width * features * features,
    )
    arrays = (av, comp_t, linear, owner, onehot)

    terms = [keep_low, got_low, got]
    for bit in bits[2:]:
        keep = sum(term.astype(F32) for term in terms)
        half = keep.shape[0] // 2
        terms = [keep[:half], swap(keep[half:].astype(BF16), bit)]
    (pair,) = call(
        layer_back_kernel,
        "layer_back",
        terms,
        [shape((piece, rank, features), BF16)],
        32 * piece * rank * features,
    )

    pairs = {0: pair}
    (total,) = table_part(0, piece, owners, False, arrays, [pair], None)
    for bit in reversed(bits[1:]):
        pairs.update({j ^ bit: swap(got, bit) for j, got in pairs.items()})
    for j in list(pairs):
        pairs[j] = after(pairs[j], total) if j else pair
        pairs[j ^ core] = swap(pairs[j], core)
    middle = [pairs[j] for j in range(1, peers - 1)]
    (total,) = table_part(1, piece, owners, False, arrays, middle, total)
    own, *sent = table_part(peers - 1, piece, owners, True, arrays, [pairs[peers - 1]], total)

    got = [swap(sent[m - 1], m, "dp") for m in range(owners - 1, 0, -1)]
    (out,) = call(finish_kernel, "finish", (own, *got), [shape(own.shape, F32)], owners * own.size)
    return out


def solution(mesh):
    placed = (
        P("dp", "dim", None),
        P("dp", "dim", None),
        P(),
        P(None, "dim"),
        P(),
        P("dp", None),
        P("dp"),
    )
    return jax.shard_map(
        shards, mesh=mesh, in_specs=placed, out_specs=P("dim", "dp"), check_vma=False
    )
```

```python
import functools

import jax
import jax.numpy as jnp
from jax import lax
from jax.experimental import pallas as pl
from jax.experimental.pallas import tpu as pltpu
from jax.sharding import PartitionSpec as P

SHARD = 256
F32, BF16 = jnp.float32, jnp.bfloat16
LIMIT = 20 * 2**20
LOAD_LIMIT = 52600 * 2**10
VMEM = pl.BlockSpec(memory_space=pltpu.VMEM)
HBM = pl.BlockSpec(memory_space=pltpu.HBM)
shape = jax.ShapeDtypeStruct


def dot_nt(a, b):
    return lax.dot_general(a, b, (((1,), (1,)), ((), ())), preferred_element_type=F32)


def dot_nn(a, b):
    return lax.dot_general(a, b, (((1,), (0,)), ((), ())), preferred_element_type=F32)


def bits_of(size):
    return [1 << t for t in range(size.bit_length() - 1)]


def halves(bits):
    numbers = [0]
    for bit in reversed(bits):
        numbers += [n ^ bit for n in numbers]
    return numbers


def call(kernel, name, args, shapes, flops, limit=LIMIT, specs=None, scratch=()):
    moved = sum(a.size * a.dtype.itemsize for a in (*args, *shapes))
    return pl.pallas_call(
        kernel,
        in_specs=specs or [VMEM] * len(args),
        out_specs=[VMEM] * len(shapes),
        out_shape=list(shapes),
        scratch_shapes=list(scratch),
        compiler_params=pltpu.CompilerParams(vmem_limit_bytes=limit),
        cost_estimate=pl.CostEstimate(flops=flops, bytes_accessed=moved, transcendentals=0),
        name=name,
    )(*args)


def load_kernel(piece, av_hbm, up_hbm, av_ref, up_ref, sems):
    me = lax.axis_index("dim")
    copies = []
    for j in range(av_ref.shape[0] // piece):
        source, to = pl.ds((me ^ j) * piece, piece), pl.ds(j * piece, piece)
        copies.append(pltpu.make_async_copy(av_hbm.at[source], av_ref.at[to], sems.at[2 * j]))
        copies.append(pltpu.make_async_copy(up_hbm.at[source], up_ref.at[to], sems.at[2 * j + 1]))
    for copy in copies:
        copy.start()
    for copy in copies:
        copy.wait()


def width_sums(comp_t_ref, proj_ref, av, up, out_ref, at):
    kind = out_ref.dtype
    rank = comp_t_ref.shape[0]
    reduced = dot_nt(comp_t_ref[...], av).astype(BF16)
    sums = dot_nn(reduced, av)
    out_ref[at, :rank] = (sums - jnp.mean(sums, axis=0, keepdims=True)).astype(kind)
    grads = dot_nn(proj_ref[...], up)
    out_ref[at, rank:] = (grads - jnp.mean(grads, axis=0, keepdims=True)).astype(kind)


def sums_kernel(orders, piece, av_ref, up_ref, comp_t_ref, proj_ref, *out_refs):
    for order, out_ref in zip(orders, out_refs):
        for n in range(len(order) * piece):
            at = order[n // piece] * piece + n % piece
            width_sums(comp_t_ref, proj_ref, av_ref[at], up_ref[at], out_ref, n)


def prepare_kernel(low, piece, av_ref, up_ref, comp_t_ref, proj_ref, mix_ref, slot_ref, out_ref, linear_ref, onehot_ref):
    sums_kernel([low], piece, av_ref, up_ref, comp_t_ref, proj_ref, out_ref)
    me = lax.axis_index("dim")
    samples, _, features = up_ref.shape
    slots = lax.broadcasted_iota(jnp.int32, (SHARD, features), 0)
    for at in range(samples):
        b = at ^ (me * piece)
        up = up_ref[at]
        linear_ref[at] = up.astype(F32) + dot_nt(up, mix_ref[...])
        hit = slots == slot_ref[:, pl.ds(pl.multiple_of(b * features, features), features)]
        onehot_ref[at * features:(at + 1) * features] = jnp.where(hit, 1.0, 0.0).T.astype(BF16)


def add_kernel(keep_ref, got_ref, out_ref):
    out_ref[...] = (keep_ref[...] + got_ref[...].astype(F32)).astype(out_ref.dtype)


def add(keep, got):
    return call(add_kernel, "add", (keep, got), [shape(keep.shape, BF16)], keep.size)[0]


def layer_back_kernel(*refs):
    *terms, pair_ref = refs
    rank = pair_ref.shape[1]
    for b in range(pair_ref.shape[0]):
        total = sum(term[b].astype(F32) for term in terms)
        centred, grads = total[:rank], total[rank:]
        inverse = 1.0 / jnp.sqrt(jnp.mean(centred * centred, axis=0, keepdims=True) + 1e-05)
        normed = centred * inverse
        moment = jnp.mean(grads * normed, axis=0, keepdims=True)
        pair_ref[b] = (inverse * (grads - normed * moment)).astype(BF16)


def lookup_mask(owner_ref, piece, features, at):
    b = at ^ (lax.axis_index("dim") * piece)
    lookups = pl.ds(pl.multiple_of(b * features, features), features)
    return owner_ref[:, lookups] ^ lax.axis_index("dp")


def spread(grad, distance, owners, masked, n):
    width, features = grad.shape
    for o, m in enumerate(owners):
        mask = jnp.where(distance == m, 1.0, 0.0).astype(BF16)
        masked[o * width:(o + 1) * width, n * features:(n + 1) * features] = grad * mask


def table_kernel(start, piece, owners, far, count, has_total, *refs):
    av_ref, comp_t_ref, linear_ref, owner_ref, onehot_ref = refs[:5]
    pair_refs, refs = refs[5:5 + count], refs[5 + count:]
    if has_total:
        total_ref, refs = refs[0], refs[1:]
    *outs, masked = refs
    _, width, features = av_ref.shape
    comp_t = comp_t_ref[...]
    for n in range(count * piece):
        at = start + n
        back = pair_refs[n // piece][n % piece]
        both = dot_nt(av_ref[at], jnp.concatenate([comp_t, back])).astype(BF16)
        grad = linear_ref[at] + dot_nn(both, jnp.concatenate([back, comp_t]))
        grad = grad.astype(BF16)
        if far:
            outs[-1][n] = grad
        spread(grad, lookup_mask(owner_ref, piece, features, at), owners, masked, n)
    added = dot_nn(masked[...], onehot_ref[start * features:(start + count * piece) * features])
    if has_total:
        added = added + total_ref[owners[0] * width:(owners[-1] + 1) * width]
    if not far:
        outs[0][...] = added
        return
    for o in range(len(owners)):
        outs[o][...] = added[o * width:(o + 1) * width].astype(outs[o].dtype)


def near_kernel(start, piece, owners, grad_ref, owner_ref, onehot_ref, total_ref, *refs):
    *outs, masked = refs
    count, width, features = grad_ref.shape
    for n in range(count):
        spread(grad_ref[n], lookup_mask(owner_ref, piece, features, start + n), owners, masked, n)
    added = dot_nn(masked[...], onehot_ref[start * features:(start + count) * features])
    added = added + total_ref[owners[0] * width:(owners[-1] + 1) * width]
    for o, out in enumerate(outs):
        out[...] = added[o * width:(o + 1) * width].astype(out.dtype)


def table_part(j, piece, owners, far, arrays, pairs, total):
    _, width, features = arrays[0].shape
    lookups = len(pairs) * piece * features
    if far:
        shapes = blocks(width, owners) + [shape((piece, width, features), BF16)]
    else:
        shapes = [shape((len(owners) * width, SHARD), F32)]
    return call(
        functools.partial(table_kernel, j * piece, piece, owners, far, len(pairs), total is not None),
        "table_part",
        [*arrays, *pairs] + ([] if total is None else [total]),
        shapes,
        2 * lookups * width * len(owners) * SHARD,
        scratch=[pltpu.VMEM((len(owners) * width, lookups), BF16)],
    )


def blocks(width, owners):
    return [shape((width, SHARD), BF16 if o else F32) for o in range(len(owners))]


def collect_kernel(*refs):
    *terms, out_ref = refs
    out_ref[...] = sum(term[...].astype(F32) for term in terms).astype(out_ref.dtype)


def swap(x, bit, axis="dim"):
    return lax.ppermute(x, axis, [(i, i ^ bit) for i in range(lax.axis_size(axis))])


def after(x, *others):
    return lax.optimization_barrier((x, *others))[0]


def shards(attribute_vectors, upstream, compress, interact_proj, linear_mix, row_owner, row_slot):
    owners, peers = lax.axis_size("dp"), lax.axis_size("dim")
    samples, width, features = attribute_vectors.shape
    rank = compress.shape[1]
    piece = samples // peers
    quarter = samples // 4
    sample_flops = 6 * width * features * rank

    bits = bits_of(peers)
    core = bits[0]
    held = halves(bits)
    count = peers // 4
    low, high = held[:count], held[count:2 * count]

    owner, slot = row_owner.reshape(1, -1), row_slot.reshape(1, -1)
    part = shape((quarter, 2 * rank, features), F32)
    comp_t, proj = compress.T, interact_proj
    av, up = call(
        functools.partial(load_kernel, piece),
        "load",
        (attribute_vectors, upstream),
        [shape(upstream.shape, BF16)] * 2,
        0,
        limit=LOAD_LIMIT,
        specs=[HBM] * 2,
        scratch=[pltpu.SemaphoreType.DMA((2 * peers,))],
    )
    args = (av, up, comp_t, proj)
    (send_high,) = call(
        functools.partial(sums_kernel, [[j ^ core for j in high]], piece),
        "first_sums",
        args,
        [shape(part.shape, BF16)],
        quarter * sample_flops,
    )
    got_high = swap(send_high, core)
    keep_high, send_low = call(
        functools.partial(sums_kernel, [high, [j ^ core for j in low]], piece),
        "sums",
        args,
        [part] * 2,
        2 * quarter * sample_flops,
    )
    got_low = swap(send_low, core)
    got = swap(add(keep_high, got_high), bits[1])
    keep_low, linear, onehot = call(
        functools.partial(prepare_kernel, low, piece),
        "prepare",
        (*args, linear_mix, slot),
        [part, shape(up.shape, F32), shape((samples * features, SHARD), BF16)],
        2 * samples * width * features * features,
    )
    arrays = (av, comp_t, linear, owner, onehot)

    terms = [keep_low, got_low, got]
    for bit in bits[2:]:
        keep = sum(term.astype(F32) for term in terms)
        half = keep.shape[0] // 2
        terms = [keep[:half], swap(keep[half:].astype(BF16), bit)]
    (pair,) = call(
        layer_back_kernel,
        "layer_back",
        terms,
        [shape((piece, rank, features), BF16)],
        32 * piece * rank * features,
    )

    pairs = {0: pair}
    everyone = list(range(owners))
    near, far = everyone[:owners // 2], everyone[owners // 2:]
    (total,) = table_part(0, piece, everyone, False, arrays, [pair], None)
    for bit in reversed(bits[1:]):
        pairs.update({j ^ bit: swap(got, bit) for j, got in pairs.items()})
    for j in list(pairs):
        pairs[j] = after(pairs[j], total) if j else pair
        pairs[j ^ core] = swap(pairs[j], core)
    middle = [pairs[j] for j in range(1, peers - 1)]
    (total,) = table_part(1, piece, everyone, False, arrays, middle, total)
    last = peers - 1
    *opposite, grad = table_part(last, piece, far, True, arrays, [pairs[last]], total)
    own = call(
        functools.partial(near_kernel, last * piece, piece, near),
        "near_part",
        (grad, owner, onehot, total),
        blocks(width, near),
        2 * piece * features * width * len(near) * SHARD,
        scratch=[pltpu.VMEM((len(near) * width, piece * features), BF16)],
    )

    def collect(terms, kind):
        return call(collect_kernel, "collect", terms, [shape((width, SHARD), kind)], width * SHARD)[0]

    steps = near[:0:-1]
    opposite = [opposite[0]] + [swap(opposite[m], m, "dp") for m in steps]
    own = [own[0]] + [swap(own[m], m, "dp") for m in steps]
    own.append(swap(collect(opposite, BF16), owners // 2, "dp"))
    return collect(own, F32)


def solution(mesh):
    placed = (
        P("dp", "dim", None),
        P("dp", "dim", None),
        P(),
        P(None, "dim"),
        P(),
        P("dp", None),
        P("dp"),
    )
    return jax.shard_map(
        shards, mesh=mesh, in_specs=placed, out_specs=P("dim", "dp"), check_vma=False
    )
```

```python
import functools

import jax
import jax.numpy as jnp
from jax import lax
from jax.experimental import pallas as pl
from jax.experimental.pallas import tpu as pltpu
from jax.sharding import PartitionSpec as P

SHARD = 256
F32, BF16 = jnp.float32, jnp.bfloat16
LIMIT = 20 * 2**20
LOAD_LIMIT = 52600 * 2**10
VMEM = pl.BlockSpec(memory_space=pltpu.VMEM)
HBM = pl.BlockSpec(memory_space=pltpu.HBM)
shape = jax.ShapeDtypeStruct


def dot_nt(a, b):
    return lax.dot_general(a, b, (((1,), (1,)), ((), ())), preferred_element_type=F32)


def dot_nn(a, b):
    return lax.dot_general(a, b, (((1,), (0,)), ((), ())), preferred_element_type=F32)


def bits_of(size):
    return [1 << t for t in range(size.bit_length() - 1)]


def halves(bits):
    numbers = [0]
    for bit in reversed(bits):
        numbers += [n ^ bit for n in numbers]
    return numbers


def call(kernel, name, args, shapes, flops, limit=LIMIT, specs=None, scratch=()):
    moved = sum(a.size * a.dtype.itemsize for a in (*args, *shapes))
    return pl.pallas_call(
        kernel,
        in_specs=specs or [VMEM] * len(args),
        out_specs=[VMEM] * len(shapes),
        out_shape=list(shapes),
        scratch_shapes=list(scratch),
        compiler_params=pltpu.CompilerParams(vmem_limit_bytes=limit),
        cost_estimate=pl.CostEstimate(flops=flops, bytes_accessed=moved, transcendentals=0),
        name=name,
    )(*args)


def load_kernel(piece, av_hbm, up_hbm, av_ref, up_ref, sems):
    me = lax.axis_index("dim")
    copies = []
    for j in range(av_ref.shape[0] // piece):
        source, to = pl.ds((me ^ j) * piece, piece), pl.ds(j * piece, piece)
        copies.append(pltpu.make_async_copy(av_hbm.at[source], av_ref.at[to], sems.at[2 * j]))
        copies.append(pltpu.make_async_copy(up_hbm.at[source], up_ref.at[to], sems.at[2 * j + 1]))
    for copy in copies:
        copy.start()
    for copy in copies:
        copy.wait()


def width_sums(comp_t_ref, proj_ref, av, up, out_ref, at):
    kind = out_ref.dtype
    rank = comp_t_ref.shape[0]
    reduced = dot_nt(comp_t_ref[...], av).astype(BF16)
    sums = dot_nn(reduced, av)
    out_ref[at, :rank] = (sums - jnp.mean(sums, axis=0, keepdims=True)).astype(kind)
    grads = dot_nn(proj_ref[...], up)
    out_ref[at, rank:] = (grads - jnp.mean(grads, axis=0, keepdims=True)).astype(kind)


def sums_kernel(orders, piece, av_ref, up_ref, comp_t_ref, proj_ref, *out_refs):
    for order, out_ref in zip(orders, out_refs):
        for n in range(len(order) * piece):
            at = order[n // piece] * piece + n % piece
            width_sums(comp_t_ref, proj_ref, av_ref[at], up_ref[at], out_ref, n)


def prepare_kernel(low, piece, av_ref, up_ref, comp_t_ref, proj_ref, mix_ref, slot_ref, out_ref, linear_ref, onehot_ref):
    sums_kernel([low], piece, av_ref, up_ref, comp_t_ref, proj_ref, out_ref)
    me = lax.axis_index("dim")
    samples, _, features = up_ref.shape
    slots = lax.broadcasted_iota(jnp.int32, (SHARD, features), 0)
    for at in range(samples):
        b = at ^ (me * piece)
        up = up_ref[at]
        linear_ref[at] = up.astype(F32) + dot_nt(up, mix_ref[...])
        hit = slots == slot_ref[:, pl.ds(pl.multiple_of(b * features, features), features)]
        onehot_ref[at * features:(at + 1) * features] = jnp.where(hit, 1.0, 0.0).T.astype(BF16)


def add_kernel(keep_ref, got_ref, out_ref):
    out_ref[...] = (keep_ref[...] + got_ref[...].astype(F32)).astype(out_ref.dtype)


def add(keep, got):
    return call(add_kernel, "add", (keep, got), [shape(keep.shape, BF16)], keep.size)[0]


def layer_back_kernel(*refs):
    *terms, pair_ref = refs
    rank = pair_ref.shape[1]
    for b in range(pair_ref.shape[0]):
        total = sum(term[b].astype(F32) for term in terms)
        centred, grads = total[:rank], total[rank:]
        inverse = 1.0 / jnp.sqrt(jnp.mean(centred * centred, axis=0, keepdims=True) + 1e-05)
        normed = centred * inverse
        moment = jnp.mean(grads * normed, axis=0, keepdims=True)
        pair_ref[b] = (inverse * (grads - normed * moment)).astype(BF16)


def lookup_mask(owner_ref, piece, features, at):
    b = at ^ (lax.axis_index("dim") * piece)
    lookups = pl.ds(pl.multiple_of(b * features, features), features)
    return owner_ref[:, lookups] ^ lax.axis_index("dp")


def spread(grad, distance, owners, masked, n):
    width, features = grad.shape
    for o, m in enumerate(owners):
        mask = jnp.where(distance == m, 1.0, 0.0).astype(BF16)
        masked[o * width:(o + 1) * width, n * features:(n + 1) * features] = grad * mask


def table_kernel(start, piece, owners, far, count, has_total, *refs):
    av_ref, comp_t_ref, linear_ref, owner_ref, onehot_ref = refs[:5]
    pair_refs, refs = refs[5:5 + count], refs[5 + count:]
    if has_total:
        total_ref, refs = refs[0], refs[1:]
    *outs, masked = refs
    _, width, features = av_ref.shape
    comp_t = comp_t_ref[...]
    for n in range(count * piece):
        at = start + n
        back = pair_refs[n // piece][n % piece]
        both = dot_nt(av_ref[at], jnp.concatenate([comp_t, back])).astype(BF16)
        grad = linear_ref[at] + dot_nn(both, jnp.concatenate([back, comp_t]))
        grad = grad.astype(BF16)
        if far:
            outs[-1][n] = grad
        spread(grad, lookup_mask(owner_ref, piece, features, at), owners, masked, n)
    added = dot_nn(masked[...], onehot_ref[start * features:(start + count * piece) * features])
    if has_total:
        added = added + total_ref[owners[0] * width:(owners[-1] + 1) * width]
    if not far:
        outs[0][...] = added
        return
    for o in range(len(owners)):
        outs[o][...] = added[o * width:(o + 1) * width].astype(outs[o].dtype)


def near_kernel(start, piece, owners, grad_ref, owner_ref, onehot_ref, total_ref, *refs):
    *outs, masked = refs
    count, width, features = grad_ref.shape
    for n in range(count):
        spread(grad_ref[n], lookup_mask(owner_ref, piece, features, start + n), owners, masked, n)
    added = dot_nn(masked[...], onehot_ref[start * features:(start + count) * features])
    added = added + total_ref[owners[0] * width:(owners[-1] + 1) * width]
    for o, out in enumerate(outs):
        out[...] = added[o * width:(o + 1) * width].astype(out.dtype)


def table_part(j, piece, owners, far, arrays, pairs, total):
    _, width, features = arrays[0].shape
    lookups = len(pairs) * piece * features
    if far:
        shapes = blocks(width, owners) + [shape((piece, width, features), BF16)]
    else:
        shapes = [shape((len(owners) * width, SHARD), F32)]
    return call(
        functools.partial(table_kernel, j * piece, piece, owners, far, len(pairs), total is not None),
        "table_part",
        [*arrays, *pairs] + ([] if total is None else [total]),
        shapes,
        2 * lookups * width * len(owners) * SHARD,
        scratch=[pltpu.VMEM((len(owners) * width, lookups), BF16)],
    )


def blocks(width, owners):
    return [shape((width, SHARD), BF16 if o else F32) for o in range(len(owners))]


def collect_kernel(*refs):
    *terms, out_ref = refs
    out_ref[...] = sum(term[...].astype(F32) for term in terms).astype(out_ref.dtype)


def swap(x, bit, axis="dim"):
    return lax.ppermute(x, axis, [(i, i ^ bit) for i in range(lax.axis_size(axis))])


def after(x, *others):
    return lax.optimization_barrier((x, *others))[0]


def shards(attribute_vectors, upstream, compress, interact_proj, linear_mix, row_owner, row_slot):
    owners, peers = lax.axis_size("dp"), lax.axis_size("dim")
    samples, width, features = attribute_vectors.shape
    rank = compress.shape[1]
    piece = samples // peers
    quarter = samples // 4
    sample_flops = 6 * width * features * rank

    bits = bits_of(peers)
    core = bits[0]
    held = halves(bits)
    count = peers // 4
    low, high = held[:count], held[count:2 * count]

    owner, slot = row_owner.reshape(1, -1), row_slot.reshape(1, -1)
    part = shape((quarter, 2 * rank, features), F32)
    comp_t, proj = compress.T, interact_proj
    av, up = call(
        functools.partial(load_kernel, piece),
        "load",
        (attribute_vectors, upstream),
        [shape(upstream.shape, BF16)] * 2,
        0,
        limit=LOAD_LIMIT,
        specs=[HBM] * 2,
        scratch=[pltpu.SemaphoreType.DMA((2 * peers,))],
    )
    args = (av, up, comp_t, proj)
    (send_high,) = call(
        functools.partial(sums_kernel, [[j ^ core for j in high]], piece),
        "first_sums",
        args,
        [shape(part.shape, BF16)],
        quarter * sample_flops,
    )
    got_high = swap(send_high, core)
    keep_high, send_low = call(
        functools.partial(sums_kernel, [high, [j ^ core for j in low]], piece),
        "sums",
        args,
        [part] * 2,
        2 * quarter * sample_flops,
    )
    got_low = swap(send_low, core)
    got = swap(add(keep_high, got_high), bits[1])
    keep_low, linear, onehot = call(
        functools.partial(prepare_kernel, low, piece),
        "prepare",
        (*args, linear_mix, slot),
        [part, shape(up.shape, F32), shape((samples * features, SHARD), BF16)],
        2 * samples * width * features * features,
    )
    arrays = (av, comp_t, linear, owner, onehot)

    terms = [keep_low, got_low, got]
    for bit in bits[2:]:
        keep = sum(term.astype(F32) for term in terms)
        half = keep.shape[0] // 2
        terms = [keep[:half], swap(keep[half:].astype(BF16), bit)]
    (pair,) = call(
        layer_back_kernel,
        "layer_back",
        terms,
        [shape((piece, rank, features), BF16)],
        32 * piece * rank * features,
    )

    pairs = {0: pair}
    everyone = list(range(owners))
    near, far = everyone[:owners // 2], everyone[owners // 2:]
    (total,) = table_part(0, piece, everyone, False, arrays, [pair], None)
    for bit in reversed(bits[1:]):
        pairs.update({j ^ bit: swap(got, bit) for j, got in pairs.items()})
    for j in list(pairs):
        pairs[j] = after(pairs[j], total) if j else pair
        pairs[j ^ core] = swap(pairs[j], core)
    middle = [pairs[j] for j in range(1, peers - 1)]
    (total,) = table_part(1, piece, everyone, False, arrays, middle, total)
    last = peers - 1
    *opposite, grad = table_part(last, piece, far, True, arrays, [pairs[last]], total)
    own = call(
        functools.partial(near_kernel, last * piece, piece, near),
        "near_part",
        (grad, owner, onehot, total),
        blocks(width, near),
        2 * piece * features * width * len(near) * SHARD,
        scratch=[pltpu.VMEM((len(near) * width, piece * features), BF16)],
    )

    def collect(terms, kind):
        return call(collect_kernel, "collect", terms, [shape((width, SHARD), kind)], width * SHARD)[0]

    steps = near[:0:-1]
    early = steps[:(len(steps) + 1) // 3]
    opposite = [opposite[0]] + [swap(opposite[m], m, "dp") for m in steps]
    terms = [own[0]] + [swap(own[m], m, "dp") for m in early]
    terms.append(swap(collect(opposite, BF16), owners // 2, "dp"))
    terms = [collect(terms, F32)] + [swap(own[m], m, "dp") for m in steps[len(early):]]
    return collect(terms, F32)


def solution(mesh):
    placed = (
        P("dp", "dim", None),
        P("dp", "dim", None),
        P(),
        P(None, "dim"),
        P(),
        P("dp", None),
        P("dp"),
    )
    return jax.shard_map(
        shards, mesh=mesh, in_specs=placed, out_specs=P("dim", "dp"), check_vma=False
    )
```

```python
import functools

import jax
import jax.numpy as jnp
from jax import lax
from jax.experimental import pallas as pl
from jax.experimental.pallas import tpu as pltpu
from jax.sharding import PartitionSpec as P

SHARD = 256
F32, BF16 = jnp.float32, jnp.bfloat16
LIMIT = 20 * 2**20
FIRST_LIMIT = 54400 * 2**10
REST_LIMIT = 52600 * 2**10
VMEM = pl.BlockSpec(memory_space=pltpu.VMEM)
HBM = pl.BlockSpec(memory_space=pltpu.HBM)
shape = jax.ShapeDtypeStruct


def dot_nt(a, b):
    return lax.dot_general(a, b, (((1,), (1,)), ((), ())), preferred_element_type=F32)


def dot_nn(a, b):
    return lax.dot_general(a, b, (((1,), (0,)), ((), ())), preferred_element_type=F32)


def bits_of(size):
    return [1 << t for t in range(size.bit_length() - 1)]


def halves(bits):
    numbers = [0]
    for bit in reversed(bits):
        numbers += [n ^ bit for n in numbers]
    return numbers


def call(kernel, name, args, shapes, flops, limit=LIMIT, specs=None, scratch=()):
    moved = sum(a.size * a.dtype.itemsize for a in (*args, *shapes))
    return pl.pallas_call(
        kernel,
        in_specs=specs or [VMEM] * len(args),
        out_specs=[VMEM] * len(shapes),
        out_shape=list(shapes),
        scratch_shapes=list(scratch),
        compiler_params=pltpu.CompilerParams(vmem_limit_bytes=limit),
        cost_estimate=pl.CostEstimate(flops=flops, bytes_accessed=moved, transcendentals=0),
        name=name,
    )(*args)


def load_kernel(order, piece, av_hbm, up_hbm, *refs):
    av_ref, up_ref, sems = refs[-3:]
    me = lax.axis_index("dim")
    copies = []
    for n, j in enumerate(order):
        source, to = pl.ds((me ^ j) * piece, piece), pl.ds(n * piece, piece)
        copies.append(pltpu.make_async_copy(av_hbm.at[source], av_ref.at[to], sems.at[2 * n]))
        copies.append(pltpu.make_async_copy(up_hbm.at[source], up_ref.at[to], sems.at[2 * n + 1]))
    for copy in copies:
        copy.start()
    for copy in copies:
        copy.wait()


def load(order, piece, av, up, limit, *others):
    part = shape((len(order) * piece, *av.shape[1:]), BF16)
    return call(
        functools.partial(load_kernel, order, piece),
        "load",
        (av, up, *others),
        [part] * 2,
        0,
        limit=limit,
        specs=[HBM] * 2 + [pl.BlockSpec(memory_space=pl.ANY)] * len(others),
        scratch=[pltpu.SemaphoreType.DMA((2 * len(order),))],
    )


def width_sums(comp_t_ref, proj_ref, av, up, out_ref, at):
    kind = out_ref.dtype
    rank = comp_t_ref.shape[0]
    reduced = dot_nt(comp_t_ref[...], av).astype(BF16)
    sums = dot_nn(reduced, av)
    out_ref[at, :rank] = (sums - jnp.mean(sums, axis=0, keepdims=True)).astype(kind)
    grads = dot_nn(proj_ref[...], up)
    out_ref[at, rank:] = (grads - jnp.mean(grads, axis=0, keepdims=True)).astype(kind)


def sums_kernel(starts, av_ref, up_ref, comp_t_ref, proj_ref, *out_refs):
    for start, out_ref in zip(starts, out_refs):
        for n in range(out_ref.shape[0]):
            width_sums(comp_t_ref, proj_ref, av_ref[start + n], up_ref[start + n], out_ref, n)


def prepare_kernel(
    order, piece, starts, first_ref, av_ref, up_ref, comp_t_ref, proj_ref, mix_ref, slot_ref, _,
    send_ref, keep_ref, linear_ref, onehot_ref,
):
    sums_kernel(starts, av_ref, up_ref, comp_t_ref, proj_ref, send_ref, keep_ref)
    me = lax.axis_index("dim")
    count, _, features = up_ref.shape
    slots = lax.broadcasted_iota(jnp.int32, (SHARD, features), 0)
    for n, j in enumerate(order):
        for s in range(piece):
            at, place = j * piece + s, n * piece + s
            b = at ^ (me * piece)
            up = up_ref[place] if place < count else first_ref[place - count]
            linear_ref[at] = up.astype(F32) + dot_nt(up, mix_ref[...])
            hit = slots == slot_ref[:, pl.ds(pl.multiple_of(b * features, features), features)]
            onehot_ref[at * features:(at + 1) * features] = jnp.where(hit, 1.0, 0.0).T.astype(BF16)


def add_kernel(keep_ref, got_ref, out_ref):
    out_ref[...] = (keep_ref[...] + got_ref[...].astype(F32)).astype(out_ref.dtype)


def add(keep, got):
    return call(add_kernel, "add", (keep, got), [shape(keep.shape, BF16)], keep.size)[0]


def layer_back_kernel(*refs):
    *terms, pair_ref = refs
    rank = pair_ref.shape[1]
    for b in range(pair_ref.shape[0]):
        total = sum(term[b].astype(F32) for term in terms)
        centred, grads = total[:rank], total[rank:]
        inverse = 1.0 / jnp.sqrt(jnp.mean(centred * centred, axis=0, keepdims=True) + 1e-05)
        normed = centred * inverse
        moment = jnp.mean(grads * normed, axis=0, keepdims=True)
        pair_ref[b] = (inverse * (grads - normed * moment)).astype(BF16)


def lookup_mask(owner_ref, piece, features, at):
    b = at ^ (lax.axis_index("dim") * piece)
    lookups = pl.ds(pl.multiple_of(b * features, features), features)
    return owner_ref[:, lookups] ^ lax.axis_index("dp")


def spread(grad, distance, owners, masked, n):
    width, features = grad.shape
    for o, m in enumerate(owners):
        mask = jnp.where(distance == m, 1.0, 0.0).astype(BF16)
        masked[o * width:(o + 1) * width, n * features:(n + 1) * features] = grad * mask


def table_kernel(order, start, piece, owners, far, count, has_total, *refs):
    rest_ref, first_ref, comp_t_ref, linear_ref, owner_ref, onehot_ref = refs[:6]
    pair_refs, refs = refs[6:6 + count], refs[6 + count:]
    if has_total:
        total_ref, refs = refs[0], refs[1:]
    *outs, masked = refs
    loaded, width, features = rest_ref.shape
    comp_t = comp_t_ref[...]
    for n in range(count * piece):
        at = start + n
        place = order.index(at // piece) * piece + at % piece
        av = rest_ref[place] if place < loaded else first_ref[place - loaded]
        back = pair_refs[n // piece][n % piece]
        both = dot_nt(av, jnp.concatenate([comp_t, back])).astype(BF16)
        grad = linear_ref[at] + dot_nn(both, jnp.concatenate([back, comp_t]))
        grad = grad.astype(BF16)
        if far:
            outs[-1][n] = grad
        spread(grad, lookup_mask(owner_ref, piece, features, at), owners, masked, n)
    added = dot_nn(masked[...], onehot_ref[start * features:(start + count * piece) * features])
    if has_total:
        added = added + total_ref[owners[0] * width:(owners[-1] + 1) * width]
    if not far:
        outs[0][...] = added
        return
    for o in range(len(owners)):
        outs[o][...] = added[o * width:(o + 1) * width].astype(outs[o].dtype)


def near_kernel(start, piece, owners, grad_ref, owner_ref, onehot_ref, total_ref, *refs):
    *outs, masked = refs
    count, width, features = grad_ref.shape
    for n in range(count):
        spread(grad_ref[n], lookup_mask(owner_ref, piece, features, start + n), owners, masked, n)
    added = dot_nn(masked[...], onehot_ref[start * features:(start + count) * features])
    added = added + total_ref[owners[0] * width:(owners[-1] + 1) * width]
    for o, out in enumerate(outs):
        out[...] = added[o * width:(o + 1) * width].astype(out.dtype)


def table_part(order, j, piece, owners, far, arrays, pairs, total):
    _, width, features = arrays[0].shape
    lookups = len(pairs) * piece * features
    if far:
        shapes = blocks(width, owners) + [shape((piece, width, features), BF16)]
    else:
        shapes = [shape((len(owners) * width, SHARD), F32)]
    return call(
        functools.partial(table_kernel, order, j * piece, piece, owners, far, len(pairs), total is not None),
        "table_part",
        [*arrays, *pairs] + ([] if total is None else [total]),
        shapes,
        2 * lookups * width * len(owners) * SHARD,
        scratch=[pltpu.VMEM((len(owners) * width, lookups), BF16)],
    )


def blocks(width, owners):
    return [shape((width, SHARD), BF16 if o else F32) for o in range(len(owners))]


def collect_kernel(*refs):
    *terms, out_ref = refs
    out_ref[...] = sum(term[...].astype(F32) for term in terms).astype(out_ref.dtype)


def swap(x, bit, axis="dim"):
    return lax.ppermute(x, axis, [(i, i ^ bit) for i in range(lax.axis_size(axis))])


def after(x, *others):
    return lax.optimization_barrier((x, *others))[0]


def shards(attribute_vectors, upstream, compress, interact_proj, linear_mix, row_owner, row_slot):
    owners, peers = lax.axis_size("dp"), lax.axis_size("dim")
    samples, width, features = attribute_vectors.shape
    rank = compress.shape[1]
    piece = samples // peers
    quarter = samples // 4
    sample_flops = 6 * width * features * rank

    bits = bits_of(peers)
    core = bits[0]
    held = halves(bits)
    count = peers // 4
    low, high = held[:count], held[count:2 * count]

    owner, slot = row_owner.reshape(1, -1), row_slot.reshape(1, -1)
    part = shape((quarter, 2 * rank, features), F32)
    comp_t, proj = compress.T, interact_proj
    first_order = [j ^ core for j in high]
    order = high + [j ^ core for j in low] + low + first_order
    first_av, first_up = load(first_order, piece, attribute_vectors, upstream, FIRST_LIMIT)
    (send_high,) = call(
        functools.partial(sums_kernel, [0]),
        "first_sums",
        (first_av, first_up, comp_t, proj),
        [shape(part.shape, BF16)],
        quarter * sample_flops,
    )
    got_high = swap(send_high, core)
    av, up = load(order[:3 * count], piece, attribute_vectors, upstream, REST_LIMIT, send_high)
    args = (av, up, comp_t, proj)
    (keep_high,) = call(
        functools.partial(sums_kernel, [0]), "sums", args, [part], quarter * sample_flops
    )
    sent = add(keep_high, got_high)
    got = swap(sent, bits[1])
    send_low, keep_low, linear, onehot = call(
        functools.partial(prepare_kernel, order, piece, [quarter, 2 * quarter]),
        "prepare",
        (first_up, *args, linear_mix, slot, sent),
        [shape(part.shape, BF16), part, shape(upstream.shape, F32), shape((samples * features, SHARD), BF16)],
        2 * samples * width * features * features,
    )
    got_low = swap(after(send_low, linear), core)
    got = after(got, keep_low)
    arrays = (av, first_av, comp_t, linear, owner, onehot)

    terms = [keep_low, got, got_low]
    for bit in bits[2:]:
        keep = sum(term.astype(F32) for term in terms)
        half = keep.shape[0] // 2
        terms = [keep[:half], swap(keep[half:].astype(BF16), bit)]
    (pair,) = call(
        layer_back_kernel,
        "layer_back",
        terms,
        [shape((piece, rank, features), BF16)],
        32 * piece * rank * features,
    )

    pairs = {0: pair}
    everyone = list(range(owners))
    near, far = everyone[:owners // 2], everyone[owners // 2:]
    (total,) = table_part(order, 0, piece, everyone, False, arrays, [pair], None)
    for bit in reversed(bits[1:]):
        pairs.update({j ^ bit: swap(got, bit) for j, got in pairs.items()})
    for j in list(pairs):
        pairs[j] = after(pairs[j], total) if j else pair
        pairs[j ^ core] = swap(pairs[j], core)
    middle = [pairs[j] for j in range(1, peers - 1)]
    (total,) = table_part(order, 1, piece, everyone, False, arrays, middle, total)
    last = peers - 1
    *opposite, grad = table_part(order, last, piece, far, True, arrays, [pairs[last]], total)
    own = call(
        functools.partial(near_kernel, last * piece, piece, near),
        "near_part",
        (grad, owner, onehot, total),
        blocks(width, near),
        2 * piece * features * width * len(near) * SHARD,
        scratch=[pltpu.VMEM((len(near) * width, piece * features), BF16)],
    )

    def collect(terms, kind):
        return call(collect_kernel, "collect", terms, [shape((width, SHARD), kind)], width * SHARD)[0]

    steps = near[:0:-1]
    opposite = [opposite[0]] + [swap(opposite[m], m, "dp") for m in steps]
    own = [own[0]] + [swap(own[m], m, "dp") for m in steps]
    own.append(swap(collect(opposite, BF16), owners // 2, "dp"))
    return collect(own, F32)


def solution(mesh):
    placed = (
        P("dp", "dim", None),
        P("dp", "dim", None),
        P(),
        P(None, "dim"),
        P(),
        P("dp", None),
        P("dp"),
    )
    return jax.shard_map(
        shards, mesh=mesh, in_specs=placed, out_specs=P("dim", "dp"), check_vma=False
    )
```

```python
import functools

import jax
import jax.numpy as jnp
from jax import lax
from jax.experimental import pallas as pl
from jax.experimental.pallas import tpu as pltpu
from jax.sharding import PartitionSpec as P

SHARD = 256
F32, BF16 = jnp.float32, jnp.bfloat16
LIMIT = 20 * 2**20
LOAD_LIMIT = 52600 * 2**10
VMEM = pl.BlockSpec(memory_space=pltpu.VMEM)
HBM = pl.BlockSpec(memory_space=pltpu.HBM)
shape = jax.ShapeDtypeStruct


def dot_nt(a, b):
    return lax.dot_general(a, b, (((1,), (1,)), ((), ())), preferred_element_type=F32)


def dot_nn(a, b):
    return lax.dot_general(a, b, (((1,), (0,)), ((), ())), preferred_element_type=F32)


def bits_of(size):
    return [1 << t for t in range(size.bit_length() - 1)]


def halves(bits):
    numbers = [0]
    for bit in reversed(bits):
        numbers += [n ^ bit for n in numbers]
    return numbers


def call(kernel, name, args, shapes, flops, limit=LIMIT, specs=None, scratch=()):
    moved = sum(a.size * a.dtype.itemsize for a in (*args, *shapes))
    return pl.pallas_call(
        kernel,
        in_specs=specs or [VMEM] * len(args),
        out_specs=[VMEM] * len(shapes),
        out_shape=list(shapes),
        scratch_shapes=list(scratch),
        compiler_params=pltpu.CompilerParams(vmem_limit_bytes=limit),
        cost_estimate=pl.CostEstimate(flops=flops, bytes_accessed=moved, transcendentals=0),
        name=name,
    )(*args)


def load_kernel(piece, av_hbm, up_hbm, av_ref, up_ref, sems):
    me = lax.axis_index("dim")
    copies = []
    for j in range(av_ref.shape[0] // piece):
        source, to = pl.ds((me ^ j) * piece, piece), pl.ds(j * piece, piece)
        copies.append(pltpu.make_async_copy(av_hbm.at[source], av_ref.at[to], sems.at[2 * j]))
        copies.append(pltpu.make_async_copy(up_hbm.at[source], up_ref.at[to], sems.at[2 * j + 1]))
    for copy in copies:
        copy.start()
    for copy in copies:
        copy.wait()


def width_sums(comp_t_ref, proj_ref, av, up, out_ref, at):
    kind = out_ref.dtype
    rank = comp_t_ref.shape[0]
    reduced = dot_nt(comp_t_ref[...], av).astype(BF16)
    sums = dot_nn(reduced, av)
    out_ref[at, :rank] = (sums - jnp.mean(sums, axis=0, keepdims=True)).astype(kind)
    grads = dot_nn(proj_ref[...], up)
    out_ref[at, rank:] = (grads - jnp.mean(grads, axis=0, keepdims=True)).astype(kind)


def sums_kernel(orders, piece, av_ref, up_ref, comp_t_ref, proj_ref, *out_refs):
    for order, out_ref in zip(orders, out_refs):
        for n in range(len(order) * piece):
            at = order[n // piece] * piece + n % piece
            width_sums(comp_t_ref, proj_ref, av_ref[at], up_ref[at], out_ref, n)


def prepare_kernel(low, piece, av_ref, up_ref, comp_t_ref, proj_ref, mix_ref, slot_ref, out_ref, linear_ref, onehot_ref):
    sums_kernel([low], piece, av_ref, up_ref, comp_t_ref, proj_ref, out_ref)
    me = lax.axis_index("dim")
    samples, _, features = up_ref.shape
    slots = lax.broadcasted_iota(jnp.int32, (SHARD, features), 0)
    for at in range(samples):
        b = at ^ (me * piece)
        up = up_ref[at]
        linear_ref[at] = up.astype(F32) + dot_nt(up, mix_ref[...])
        hit = slots == slot_ref[:, pl.ds(pl.multiple_of(b * features, features), features)]
        onehot_ref[at * features:(at + 1) * features] = jnp.where(hit, 1.0, 0.0).T.astype(BF16)


def add_kernel(keep_ref, got_ref, out_ref):
    out_ref[...] = (keep_ref[...] + got_ref[...].astype(F32)).astype(out_ref.dtype)


def add(keep, got):
    return call(add_kernel, "add", (keep, got), [shape(keep.shape, BF16)], keep.size)[0]


def layer_back_kernel(*refs):
    *terms, pair_ref = refs
    rank = pair_ref.shape[1]
    for b in range(pair_ref.shape[0]):
        total = sum(term[b].astype(F32) for term in terms)
        centred, grads = total[:rank], total[rank:]
        inverse = 1.0 / jnp.sqrt(jnp.mean(centred * centred, axis=0, keepdims=True) + 1e-05)
        normed = centred * inverse
        moment = jnp.mean(grads * normed, axis=0, keepdims=True)
        pair_ref[b] = (inverse * (grads - normed * moment)).astype(BF16)


def lookup_mask(owner_ref, piece, features, at):
    b = at ^ (lax.axis_index("dim") * piece)
    lookups = pl.ds(pl.multiple_of(b * features, features), features)
    return owner_ref[:, lookups] ^ lax.axis_index("dp")


def spread(grad, distance, owners, masked, n):
    width, features = grad.shape
    for o, m in enumerate(owners):
        mask = jnp.where(distance == m, 1.0, 0.0).astype(BF16)
        masked[o * width:(o + 1) * width, n * features:(n + 1) * features] = grad * mask


def table_kernel(start, piece, owners, far, count, has_total, *refs):
    av_ref, comp_t_ref, linear_ref, owner_ref, onehot_ref = refs[:5]
    pair_refs, refs = refs[5:5 + count], refs[5 + count:]
    if has_total:
        total_ref, refs = refs[0], refs[1:]
    *outs, masked = refs
    _, width, features = av_ref.shape
    comp_t = comp_t_ref[...]
    for n in range(count * piece):
        at = start + n
        back = pair_refs[n // piece][n % piece]
        both = dot_nt(av_ref[at], jnp.concatenate([comp_t, back])).astype(BF16)
        grad = linear_ref[at] + dot_nn(both, jnp.concatenate([back, comp_t]))
        grad = grad.astype(BF16)
        if far:
            outs[-1][n] = grad
        spread(grad, lookup_mask(owner_ref, piece, features, at), owners, masked, n)
    added = dot_nn(masked[...], onehot_ref[start * features:(start + count * piece) * features])
    if has_total:
        added = added + total_ref[owners[0] * width:(owners[-1] + 1) * width]
    if not far:
        outs[0][...] = added
        return
    for o in range(len(owners)):
        outs[o][...] = added[o * width:(o + 1) * width].astype(outs[o].dtype)


def near_kernel(start, piece, owners, grad_ref, owner_ref, onehot_ref, total_ref, *refs):
    *outs, masked = refs
    count, width, features = grad_ref.shape
    for n in range(count):
        spread(grad_ref[n], lookup_mask(owner_ref, piece, features, start + n), owners, masked, n)
    added = dot_nn(masked[...], onehot_ref[start * features:(start + count) * features])
    added = added + total_ref[owners[0] * width:(owners[-1] + 1) * width]
    for o, out in enumerate(outs):
        out[...] = added[o * width:(o + 1) * width].astype(out.dtype)


def table_part(j, piece, owners, far, arrays, pairs, total):
    _, width, features = arrays[0].shape
    lookups = len(pairs) * piece * features
    if far:
        shapes = blocks(width, owners) + [shape((piece, width, features), BF16)]
    else:
        shapes = [shape((len(owners) * width, SHARD), F32)]
    return call(
        functools.partial(table_kernel, j * piece, piece, owners, far, len(pairs), total is not None),
        "table_part",
        [*arrays, *pairs] + ([] if total is None else [total]),
        shapes,
        2 * lookups * width * len(owners) * SHARD,
        scratch=[pltpu.VMEM((len(owners) * width, lookups), BF16)],
    )


def blocks(width, owners):
    return [shape((width, SHARD), BF16 if o else F32) for o in range(len(owners))]


def collect_kernel(*refs):
    *terms, out_ref = refs
    out_ref[...] = sum(term[...].astype(F32) for term in terms).astype(out_ref.dtype)


def swap(x, bit, axis="dim"):
    return lax.ppermute(x, axis, [(i, i ^ bit) for i in range(lax.axis_size(axis))])


def after(x, *others):
    return lax.optimization_barrier((x, *others))[0]


def shards(attribute_vectors, upstream, compress, interact_proj, linear_mix, row_owner, row_slot):
    owners, peers = lax.axis_size("dp"), lax.axis_size("dim")
    samples, width, features = attribute_vectors.shape
    rank = compress.shape[1]
    piece = samples // peers
    quarter = samples // 4
    sample_flops = 6 * width * features * rank

    bits = bits_of(peers)
    core = bits[0]
    held = halves(bits)
    count = peers // 4
    low, high = held[:count], held[count:2 * count]

    owner, slot = row_owner.reshape(1, -1), row_slot.reshape(1, -1)
    part = shape((quarter, 2 * rank, features), F32)
    comp_t, proj = compress.T, interact_proj
    av, up = call(
        functools.partial(load_kernel, piece),
        "load",
        (attribute_vectors, upstream),
        [shape(upstream.shape, BF16)] * 2,
        0,
        limit=LOAD_LIMIT,
        specs=[HBM] * 2,
        scratch=[pltpu.SemaphoreType.DMA((2 * peers,))],
    )
    args = (av, up, comp_t, proj)
    (send_high,) = call(
        functools.partial(sums_kernel, [[j ^ core for j in high]], piece),
        "first_sums",
        args,
        [shape(part.shape, BF16)],
        quarter * sample_flops,
    )
    got_high = swap(send_high, core)
    keep_high, send_low = call(
        functools.partial(sums_kernel, [high, [j ^ core for j in low]], piece),
        "sums",
        args,
        [part] * 2,
        2 * quarter * sample_flops,
    )
    got_low = swap(send_low, core)
    got = swap(add(keep_high, got_high), bits[1])
    keep_low, linear, onehot = call(
        functools.partial(prepare_kernel, low, piece),
        "prepare",
        (*args, linear_mix, slot),
        [part, shape(up.shape, F32), shape((samples * features, SHARD), BF16)],
        2 * samples * width * features * features,
    )
    arrays = (av, comp_t, linear, owner, onehot)

    terms = [keep_low, got_low, got]
    for bit in bits[2:]:
        keep = sum(term.astype(F32) for term in terms)
        half = keep.shape[0] // 2
        terms = [keep[:half], swap(keep[half:].astype(BF16), bit)]
    (pair,) = call(
        layer_back_kernel,
        "layer_back",
        terms,
        [shape((piece, rank, features), BF16)],
        32 * piece * rank * features,
    )

    pairs = {0: pair}
    everyone = list(range(owners))
    near, far = everyone[:owners // 2], everyone[owners // 2:]
    (total,) = table_part(0, piece, everyone, False, arrays, [pair], None)
    for bit in reversed(bits[1:]):
        pairs.update({j ^ bit: swap(got, bit) for j, got in pairs.items()})
    for j in list(pairs):
        pairs[j] = after(pairs[j], total) if j else pair
        pairs[j ^ core] = swap(pairs[j], core)
    middle = [pairs[j] for j in range(1, peers - 1)]
    (total,) = table_part(1, piece, everyone, False, arrays, middle, total)
    last = peers - 1
    *opposite, grad = table_part(last, piece, far, True, arrays, [pairs[last]], total)
    own = call(
        functools.partial(near_kernel, last * piece, piece, near),
        "near_part",
        (grad, owner, onehot, total),
        blocks(width, near),
        2 * piece * features * width * len(near) * SHARD,
        scratch=[pltpu.VMEM((len(near) * width, piece * features), BF16)],
    )

    def collect(terms, kind):
        return call(collect_kernel, "collect", terms, [shape((width, SHARD), kind)], width * SHARD)[0]

    steps = near[:0:-1]
    early = steps[:-1]
    opposite = [opposite[0]] + [swap(opposite[m], m, "dp") for m in steps]
    terms = [own[0]] + [swap(own[m], m, "dp") for m in early]
    terms.append(swap(collect(opposite, BF16), owners // 2, "dp"))
    terms = [collect(terms, F32)] + [swap(own[m], m, "dp") for m in steps[len(early):]]
    return collect(terms, F32)


def solution(mesh):
    placed = (
        P("dp", "dim", None),
        P("dp", "dim", None),
        P(),
        P(None, "dim"),
        P(),
        P("dp", None),
        P("dp"),
    )
    return jax.shard_map(
        shards, mesh=mesh, in_specs=placed, out_specs=P("dim", "dp"), check_vma=False
    )
```

```python
import functools

import jax
import jax.numpy as jnp
from jax import lax
from jax.experimental import pallas as pl
from jax.experimental.pallas import tpu as pltpu
from jax.sharding import PartitionSpec as P

SHARD = 256
F32, BF16 = jnp.float32, jnp.bfloat16
LIMIT = 20 * 2**20
LOAD_LIMIT = 52600 * 2**10
VMEM = pl.BlockSpec(memory_space=pltpu.VMEM)
HBM = pl.BlockSpec(memory_space=pltpu.HBM)
shape = jax.ShapeDtypeStruct


def dot_nt(a, b):
    return lax.dot_general(a, b, (((1,), (1,)), ((), ())), preferred_element_type=F32)


def dot_nn(a, b):
    return lax.dot_general(a, b, (((1,), (0,)), ((), ())), preferred_element_type=F32)


def bits_of(size):
    return [1 << t for t in range(size.bit_length() - 1)]


def halves(bits):
    numbers = [0]
    for bit in reversed(bits):
        numbers += [n ^ bit for n in numbers]
    return numbers


def call(kernel, name, args, shapes, flops, limit=LIMIT, specs=None, scratch=()):
    moved = sum(a.size * a.dtype.itemsize for a in (*args, *shapes))
    return pl.pallas_call(
        kernel,
        in_specs=specs or [VMEM] * len(args),
        out_specs=[VMEM] * len(shapes),
        out_shape=list(shapes),
        scratch_shapes=list(scratch),
        compiler_params=pltpu.CompilerParams(vmem_limit_bytes=limit),
        cost_estimate=pl.CostEstimate(flops=flops, bytes_accessed=moved, transcendentals=0),
        name=name,
    )(*args)


def load_kernel(piece, av_hbm, up_hbm, av_ref, up_ref, sems):
    me = lax.axis_index("dim")
    copies = []
    for j in range(av_ref.shape[0] // piece):
        source, to = pl.ds((me ^ j) * piece, piece), pl.ds(j * piece, piece)
        copies.append(pltpu.make_async_copy(av_hbm.at[source], av_ref.at[to], sems.at[2 * j]))
        copies.append(pltpu.make_async_copy(up_hbm.at[source], up_ref.at[to], sems.at[2 * j + 1]))
    for copy in copies:
        copy.start()
    for copy in copies:
        copy.wait()


def width_sums(comp_t_ref, proj_ref, av, up, out_ref, at):
    kind = out_ref.dtype
    rank = comp_t_ref.shape[0]
    reduced = dot_nt(comp_t_ref[...], av).astype(BF16)
    sums = dot_nn(reduced, av)
    out_ref[at, :rank] = (sums - jnp.mean(sums, axis=0, keepdims=True)).astype(kind)
    grads = dot_nn(proj_ref[...], up)
    out_ref[at, rank:] = (grads - jnp.mean(grads, axis=0, keepdims=True)).astype(kind)


def sums_kernel(orders, piece, av_ref, up_ref, comp_t_ref, proj_ref, *out_refs):
    for order, out_ref in zip(orders, out_refs):
        for n in range(len(order) * piece):
            at = order[n // piece] * piece + n % piece
            width_sums(comp_t_ref, proj_ref, av_ref[at], up_ref[at], out_ref, n)


def prepare_kernel(low, piece, av_ref, up_ref, comp_t_ref, proj_ref, mix_ref, slot_ref, out_ref, linear_ref, onehot_ref):
    sums_kernel([low], piece, av_ref, up_ref, comp_t_ref, proj_ref, out_ref)
    me = lax.axis_index("dim")
    samples, _, features = up_ref.shape
    slots = lax.broadcasted_iota(jnp.int32, (SHARD, features), 0)
    for at in range(samples):
        b = at ^ (me * piece)
        up = up_ref[at]
        linear_ref[at] = up.astype(F32) + dot_nt(up, mix_ref[...])
        hit = slots == slot_ref[:, pl.ds(pl.multiple_of(b * features, features), features)]
        onehot_ref[at * features:(at + 1) * features] = jnp.where(hit, 1.0, 0.0).T.astype(BF16)


def add_kernel(keep_ref, got_ref, out_ref):
    out_ref[...] = (keep_ref[...] + got_ref[...].astype(F32)).astype(out_ref.dtype)


def add(keep, got):
    return call(add_kernel, "add", (keep, got), [shape(keep.shape, BF16)], keep.size)[0]


def layer_back_kernel(*refs):
    *terms, pair_ref = refs
    rank = pair_ref.shape[1]
    for b in range(pair_ref.shape[0]):
        total = sum(term[b].astype(F32) for term in terms)
        centred, grads = total[:rank], total[rank:]
        inverse = 1.0 / jnp.sqrt(jnp.mean(centred * centred, axis=0, keepdims=True) + 1e-05)
        normed = centred * inverse
        moment = jnp.mean(grads * normed, axis=0, keepdims=True)
        pair_ref[b] = (inverse * (grads - normed * moment)).astype(BF16)


def lookup_mask(owner_ref, piece, features, at):
    b = at ^ (lax.axis_index("dim") * piece)
    lookups = pl.ds(pl.multiple_of(b * features, features), features)
    return owner_ref[:, lookups] ^ lax.axis_index("dp")


def spread(grad, distance, owners, masked, n):
    width, features = grad.shape
    for o, m in enumerate(owners):
        mask = jnp.where(distance == m, 1.0, 0.0).astype(BF16)
        masked[o * width:(o + 1) * width, n * features:(n + 1) * features] = grad * mask


def table_kernel(start, piece, owners, far, count, has_total, *refs):
    av_ref, comp_t_ref, linear_ref, owner_ref, onehot_ref = refs[:5]
    pair_refs, refs = refs[5:5 + count], refs[5 + count:]
    if has_total:
        total_ref, refs = refs[0], refs[1:]
    *outs, masked = refs
    _, width, features = av_ref.shape
    comp_t = comp_t_ref[...]
    for n in range(count * piece):
        at = start + n
        back = pair_refs[n // piece][n % piece]
        both = dot_nt(av_ref[at], jnp.concatenate([comp_t, back])).astype(BF16)
        grad = linear_ref[at] + dot_nn(both, jnp.concatenate([back, comp_t]))
        grad = grad.astype(BF16)
        spread(grad, lookup_mask(owner_ref, piece, features, at), owners, masked, n)
    added = dot_nn(masked[...], onehot_ref[start * features:(start + count * piece) * features])
    if has_total:
        added = added + total_ref[owners[0] * width:(owners[-1] + 1) * width]
    if not far:
        outs[0][...] = added
        return
    half = len(owners) // 2
    for o in range(half):
        mine, opposite = (added[m * width:(m + 1) * width] for m in (o, half + o))
        if o:
            outs[o + 1][0] = opposite.astype(BF16)
            outs[o + 1][1] = mine.astype(BF16)
        else:
            outs[0][...] = mine
            outs[1][...] = opposite


def table_part(j, piece, owners, far, arrays, pairs, total):
    _, width, features = arrays[0].shape
    lookups = len(pairs) * piece * features
    if far:
        kept, sent = shape((width, SHARD), F32), shape((2, width, SHARD), BF16)
        shapes = [kept] * 2 + [sent] * (len(owners) // 2 - 1)
    else:
        shapes = [shape((len(owners) * width, SHARD), F32)]
    return call(
        functools.partial(table_kernel, j * piece, piece, owners, far, len(pairs), total is not None),
        "table_part",
        [*arrays, *pairs] + ([] if total is None else [total]),
        shapes,
        2 * lookups * width * len(owners) * SHARD,
        scratch=[pltpu.VMEM((len(owners) * width, lookups), BF16)],
    )


def collect_kernel(at, *refs):
    *terms, out_ref = refs
    terms = [(term[at] if len(term.shape) == 3 else term[...]).astype(F32) for term in terms]
    out_ref[...] = sum(terms).astype(out_ref.dtype)


def swap(x, bit, axis="dim"):
    return lax.ppermute(x, axis, [(i, i ^ bit) for i in range(lax.axis_size(axis))])


def after(x, *others):
    return lax.optimization_barrier((x, *others))[0]


def shards(attribute_vectors, upstream, compress, interact_proj, linear_mix, row_owner, row_slot):
    owners, peers = lax.axis_size("dp"), lax.axis_size("dim")
    samples, width, features = attribute_vectors.shape
    rank = compress.shape[1]
    piece = samples // peers
    quarter = samples // 4
    sample_flops = 6 * width * features * rank

    bits = bits_of(peers)
    core = bits[0]
    held = halves(bits)
    count = peers // 4
    low, high = held[:count], held[count:2 * count]

    owner, slot = row_owner.reshape(1, -1), row_slot.reshape(1, -1)
    part = shape((quarter, 2 * rank, features), F32)
    comp_t, proj = compress.T, interact_proj
    av, up = call(
        functools.partial(load_kernel, piece),
        "load",
        (attribute_vectors, upstream),
        [shape(upstream.shape, BF16)] * 2,
        0,
        limit=LOAD_LIMIT,
        specs=[HBM] * 2,
        scratch=[pltpu.SemaphoreType.DMA((2 * peers,))],
    )
    args = (av, up, comp_t, proj)
    (send_high,) = call(
        functools.partial(sums_kernel, [[j ^ core for j in high]], piece),
        "first_sums",
        args,
        [shape(part.shape, BF16)],
        quarter * sample_flops,
    )
    got_high = swap(send_high, core)
    keep_high, send_low = call(
        functools.partial(sums_kernel, [high, [j ^ core for j in low]], piece),
        "sums",
        args,
        [part] * 2,
        2 * quarter * sample_flops,
    )
    got_low = swap(send_low, core)
    got = swap(add(keep_high, got_high), bits[1])
    keep_low, linear, onehot = call(
        functools.partial(prepare_kernel, low, piece),
        "prepare",
        (*args, linear_mix, slot),
        [part, shape(up.shape, F32), shape((samples * features, SHARD), BF16)],
        2 * samples * width * features * features,
    )
    arrays = (av, comp_t, linear, owner, onehot)

    terms = [keep_low, got_low, got]
    for bit in bits[2:]:
        keep = sum(term.astype(F32) for term in terms)
        half = keep.shape[0] // 2
        terms = [keep[:half], swap(keep[half:].astype(BF16), bit)]
    (pair,) = call(
        layer_back_kernel,
        "layer_back",
        terms,
        [shape((piece, rank, features), BF16)],
        32 * piece * rank * features,
    )

    pairs = {0: pair}
    everyone = list(range(owners))
    (total,) = table_part(0, piece, everyone, False, arrays, [pair], None)
    for bit in reversed(bits[1:]):
        pairs.update({j ^ bit: swap(got, bit) for j, got in pairs.items()})
    for j in list(pairs):
        pairs[j] = after(pairs[j], total) if j else pair
        pairs[j ^ core] = swap(pairs[j], core)
    middle = [pairs[j] for j in range(1, peers - 1)]
    (total,) = table_part(1, piece, everyone, False, arrays, middle, total)
    last = peers - 1
    own, opposite, *sent = table_part(last, piece, everyone, True, arrays, [pairs[last]], total)

    def collect(at, terms, kind):
        kernel = functools.partial(collect_kernel, at)
        return call(kernel, "collect", terms, [shape((width, SHARD), kind)], width * SHARD)[0]

    got = [swap(sent[m - 1], m, "dp") for m in range(owners // 2 - 1, 0, -1)]
    across = swap(collect(0, [opposite, *got], BF16), owners // 2, "dp")
    return collect(1, [own, *got, across], F32)


def solution(mesh):
    placed = (
        P("dp", "dim", None),
        P("dp", "dim", None),
        P(),
        P(None, "dim"),
        P(),
        P("dp", None),
        P("dp"),
    )
    return jax.shard_map(
        shards, mesh=mesh, in_specs=placed, out_specs=P("dim", "dp"), check_vma=False
    )
```
